32 devices in a mesh: lat: 8 (over z, x), lon: 4 (over y, core).
Axes of the slice: x: 2, y: 2, z: 4, core: 2. Of those that a mesh axis runs over, the one named last changes fastest.
Arguments:
- tracer: float32 [32, 192, 1152], P(None, 'lat', 'lon'), may hold values from -6 to 6
- wind_u: float32 [32, 192, 1152], P(None, 'lat', 'lon'), may hold values from -2.5 to 2.5
- wind_v: float32 [32, 192, 1152], P(None, 'lat', 'lon'), may hold values from -2.5 to 2.5
- ocean_temp: float32 [4, 256, 3584], P(None, 'lat', 'lon'), may hold values from -6 to 6
- land_mask: int32 [256, 3584], P('lat', 'lon'), may hold values 0 or 1
- remap_rows: int32 [256, 3584], P('lat', 'lon'), may hold values from 0 to 191, as said below
- remap_cols: int32 [256, 3584], P('lat', 'lon'), may hold values from 0 to 1151, as said below
- polar_rows: int32 [24], replicated, may hold values from 0 to 191, as said below
Outputs:
- tracer_out: float32 [32, 192, 1152], P(None, 'lat', 'lon')
- ocean_out: float32 [4, 256, 3584], P(None, 'lat', 'lon')
The draws below stay inside these ranges and needn't reach their ends.
Inputs may be any that keep to these rules, and one draw needn't show every extreme that they name: `remap_rows`: for an ocean cell in row block b of 32 rows, an atmosphere row from b * 24 - 1 to (b + 1) * 24, within the grid. `remap_cols`: for an ocean cell in column block c of 896 columns, an atmosphere column from c * 288 - 1 to (c + 1) * 288, modulo 1152. `polar_rows`: distinct rows, each among the 24 rows nearest either pole.
All inputs are finite; a program needn't handle non-finite values. No bound on the sum of `land_mask` on one device may be relied on, other than what follows from the above.
Results may differ from the reference program's by a relative error of at most 0.0001.
Values sent between devices are 32-bit elements; how exact they have to be, the bound alone decides.
A program may use at most 128 MiB of HBM per device.

```python
import math
import jax
import jax.numpy as jnp

NLON = 1152
ROWS = 24
LEV = 32
STEPS = 2
OSTEPS = 2
OLEV = 4
OROWS = 32
OCOLS = 896
NLAT = 192
LON_DEV = 288
BAND = 24
ONY = 256
ONX = 3584


def draw_remap_rows(key, part):
    base_row = jnp.arange(ONY, dtype=jnp.int32)[:, None] // OROWS * ROWS - 1
    offset = jax.random.randint(key, (ONY, ONX), 0, ROWS + 2)
    return jnp.clip(base_row + offset, 0, NLAT - 1).astype(jnp.int32)


def draw_remap_cols(key, part):
    base_col = jnp.arange(ONX, dtype=jnp.int32)[None, :] // OCOLS * LON_DEV - 1
    offset = jax.random.randint(key, (ONY, ONX), 0, LON_DEV + 2)
    return ((base_col + offset) % NLON).astype(jnp.int32)


def draw_polar_rows(key, part):
    band_index = jnp.arange(2 * BAND, dtype=jnp.int32)
    band_row = jnp.where(band_index < BAND, band_index, NLAT - 2 * BAND + band_index)
    order = jax.random.permutation(key, 2 * BAND)
    return band_row[order[:BAND]].astype(jnp.int32)


def place_ends(array, stream_key, smallest, top_value):
    spot = [jax.random.randint(jax.random.fold_in(stream_key, axis), (), 0, length) for axis, length in enumerate(array.shape)]
    widest = array.shape.index(max(array.shape))
    beside = spot[:widest] + [(spot[widest] + 1) % array.shape[widest]] + spot[widest + 1:]
    return array.at[tuple(spot)].set(smallest).at[tuple(beside)].set(top_value)


def block_scale(key, extent, pieces, low, top_value):
    def one(axis_at, parts):
        heights = jax.random.uniform(jax.random.fold_in(jax.random.fold_in(key, 6), axis_at), (parts,), jnp.float32, low / len(pieces), top_value / len(pieces))
        return jnp.repeat(jnp.exp(heights), extent[axis_at] // parts).reshape((-1,) + (1,) * (len(extent) - axis_at - 1))

    factor_of = one(*pieces[0])
    for cut in pieces[1:]:
        factor_of = factor_of * one(*cut)
    return factor_of


def bell_draw(key, shape, deviation, most, split=(), kind=jnp.bfloat16):
    array = jax.random.normal(key, shape, jnp.float32) * deviation
    if len(split) > 0:
        array = block_scale(key, shape, split, -0.22, 0.18) * array
    return jnp.clip(array, min=-most, max=most).astype(kind)


def setup_inputs(seed: int = 0) -> dict:
    arg_keys = jax.random.split(jax.random.key(seed), 9)
    tracer = bell_draw(arg_keys[0], (LEV, NLAT, NLON), 1.0, 6.0, ((1, 8), (2, 4)), jnp.float32)
    wind_u = bell_draw(arg_keys[1], (LEV, NLAT, NLON), 0.4, 2.5, ((1, 8), (2, 4)), jnp.float32)
    wind_v = bell_draw(arg_keys[2], (LEV, NLAT, NLON), 0.4, 2.5, ((1, 8), (2, 4)), jnp.float32)
    ocean_temp = bell_draw(arg_keys[3], (OLEV, ONY, ONX), 1.0, 6.0, ((1, 8), (2, 4)), jnp.float32)
    land_mask = place_ends((jax.random.randint(arg_keys[4], (ONY, ONX), 0, 10) < 7).astype(jnp.int32), jax.random.fold_in(arg_keys[4], 1), 0, 1)
    remap_rows = draw_remap_rows(jax.random.fold_in(arg_keys[8], 71), 0)
    remap_cols = draw_remap_cols(jax.random.fold_in(arg_keys[8], 71), 0)
    polar_rows = draw_polar_rows(jax.random.fold_in(arg_keys[8], 71), 0)
    return dict(tracer=tracer, wind_u=wind_u, wind_v=wind_v, ocean_temp=ocean_temp, land_mask=land_mask, remap_rows=remap_rows, remap_cols=remap_cols, polar_rows=polar_rows)


advect_coef = 0.2
diffuse_coef = 0.1
flux_coef = 0.25
ocean_diffuse = 0.15
vertical_mix = 0.2


def damp_table(row_index, polar_rows, wave_numbers):
    latitude_cos = jnp.sin(math.pi * (row_index.astype(jnp.float32) + 0.5) / NLAT)
    ratio = latitude_cos / math.sin(math.pi * BAND / NLAT)
    wave_sine = jnp.sin(math.pi * wave_numbers / NLON)
    safe_sine = jnp.where(wave_numbers > 0.5, wave_sine, 1.0)
    damping = jnp.where(wave_numbers[None, :] > 0.5, jnp.minimum(1.0, ratio[:, None] / safe_sine[None, :]), 1.0)
    listed = jnp.any(row_index[:, None] == polar_rows[None, :], axis=1)
    return jnp.where(listed[:, None], damping, 1.0)


def north_of(field):
    return jnp.concatenate([field[..., 1:, :], jnp.zeros_like(field[..., :1, :])], axis=-2)


def south_of(field):
    return jnp.concatenate([jnp.zeros_like(field[..., :1, :]), field[..., :-1, :]], axis=-2)


def atmos_step(tracer_now, wind_u, wind_v):
    east_side = jnp.roll(tracer_now, -1, axis=-1)
    west_side = jnp.roll(tracer_now, 1, axis=-1)
    north_side = north_of(tracer_now)
    south_side = south_of(tracer_now)
    advect = wind_u * (east_side - west_side) + wind_v * (north_side - south_side)
    spread_sum = east_side + west_side + north_side + south_side - 4.0 * tracer_now
    return tracer_now - advect_coef * advect + diffuse_coef * spread_sum


def ocean_step(temp, sea, air_temp, air_speed):
    top_level = temp[0] + sea * flux_coef * air_speed * (air_temp - temp[0])
    temp = jnp.concatenate([top_level[None], temp[1:]], axis=0)
    lateral = sea * (jnp.roll(sea, -1, axis=-1) * (jnp.roll(temp, -1, axis=-1) - temp)
                     + jnp.roll(sea, 1, axis=-1) * (jnp.roll(temp, 1, axis=-1) - temp)
                     + north_of(sea) * (north_of(temp) - temp)
                     + south_of(sea) * (south_of(temp) - temp))
    temp = temp + ocean_diffuse * lateral
    upper = jnp.concatenate([temp[:1], temp[:-1]], axis=0)
    lower = jnp.concatenate([temp[1:], temp[-1:]], axis=0)
    return temp + vertical_mix * sea * (upper + lower - 2.0 * temp)


def reference(tracer, wind_u, wind_v, ocean_temp, land_mask, remap_rows, remap_cols, polar_rows):
    wave_numbers = jnp.arange(NLON // 2 + 1).astype(jnp.float32)
    table = damp_table(jnp.arange(NLAT).astype(jnp.int32), polar_rows, wave_numbers)
    tracer_now = tracer
    for step_index in range(STEPS):
        tracer_now = atmos_step(tracer_now, wind_u, wind_v)
        spectrum = jnp.fft.rfft(tracer_now, axis=2)
        tracer_now = jnp.fft.irfft(spectrum * table[None], n=NLON, axis=2).astype(tracer.dtype)
    bottom_temp = tracer_now[LEV - 1]
    bottom_speed = jnp.abs(wind_u[LEV - 1]) + jnp.abs(wind_v[LEV - 1]) + 0.5
    air_temp = bottom_temp[remap_rows, remap_cols]
    air_speed = bottom_speed[remap_rows, remap_cols]
    sea = land_mask.astype(jnp.float32)
    temp = ocean_temp
    for step_index in range(OSTEPS):
        temp = ocean_step(temp, sea, air_temp, air_speed)
    return tracer_now, temp
```

```python
import functools
import math

import jax
import jax.numpy as jnp
import ml_dtypes
import numpy as np
from jax import lax
from jax.experimental import pallas as pl
from jax.experimental.pallas import tpu as pltpu
from jax.sharding import PartitionSpec as P

STEPS = 2
OSTEPS = 2
MESH = pl.DeviceIdType.MESH
VMEM = pl.BlockSpec(memory_space=pltpu.VMEM)

advect_coef = 0.2
diffuse_coef = 0.1
flux_coef = 0.25
ocean_diffuse = 0.15
vertical_mix = 0.2


def params(cid=None):
    if cid is None:
        return pltpu.CompilerParams(vmem_limit_bytes=48 * 2**20)
    return pltpu.CompilerParams(
        collective_id=cid, has_side_effects=True, vmem_limit_bytes=48 * 2**20
    )


def split_basis(matrix):
    high = matrix.astype(ml_dtypes.bfloat16)
    low = (matrix - high.astype(np.float64)).astype(ml_dtypes.bfloat16)
    return high, low


def make_bases(lon_total):
    quarter = lon_total // 4
    n = np.arange(quarter)[:, None]

    def angle(k):
        return 2.0 * math.pi * ((n * k[None, :]) % lon_total) / lon_total

    k0 = 4 * np.arange(quarter // 2 + 1)
    k0s = 4 * np.arange(1, quarter // 2)
    m0 = np.concatenate([np.cos(angle(k0)), np.sin(angle(k0s))], axis=1)
    kk0 = np.concatenate([k0, k0s])
    s0 = np.where((kk0 == 0) | (kk0 == lon_total // 2), 1.0 / quarter, 2.0 / quarter)
    k2 = 4 * np.arange(quarter // 2) + 2
    m2 = np.concatenate([np.cos(angle(k2)), np.sin(angle(k2))], axis=1)
    kk2 = np.concatenate([k2, k2])
    s2 = np.full(quarter, 2.0 / quarter)
    k1 = 4 * np.arange(quarter) + 1
    cos1, sin1 = np.cos(angle(k1)), np.sin(angle(k1))
    m1 = np.concatenate(
        [np.concatenate([cos1, -sin1], axis=1), np.concatenate([-sin1, -cos1], axis=1)], axis=0
    )
    f1 = np.minimum(k1, lon_total - k1)
    kk1 = np.concatenate([f1, f1])
    s1 = np.full(2 * quarter, 1.0 / quarter)
    waves = np.concatenate([kk0, kk2, kk1]).astype(np.float32)
    scale = np.concatenate([s0 / 4, s2 / 4, s1 / 2]).astype(np.float32)
    return (m0, m2, m1), waves, scale


def damp_table(row_index, polar_rows, wave_numbers, lat_total, band_rows, lon_total):
    latitude_cos = jnp.sin(math.pi * (row_index.astype(jnp.float32) + 0.5) / lat_total)
    ratio = latitude_cos / math.sin(math.pi * band_rows / lat_total)
    wave_sine = jnp.sin(math.pi * wave_numbers / lon_total)
    safe_sine = jnp.where(wave_numbers > 0.5, wave_sine, 1.0)
    damping = jnp.where(
        wave_numbers[None, :] > 0.5, jnp.minimum(1.0, ratio[:, None] / safe_sine[None, :]), 1.0
    )
    listed = jnp.any(row_index[:, None] == polar_rows[None, :], axis=1)
    return jnp.where(listed[:, None], damping, 1.0)


def peer_copy(src, dst, send_sem, recv_sem, lat, lon):
    return pltpu.make_async_remote_copy(
        src_ref=src, dst_ref=dst, send_sem=send_sem, recv_sem=recv_sem,
        device_id=(lat, lon), device_id_type=MESH,
    )


def edges_kernel(lat_n, lon_n, last_row, first_row, last_col, first_col,
                 south, north, west, east, send, recv):
    lat, lon = lax.axis_index("lat"), lax.axis_index("lon")
    right, left = lax.rem(lon + 1, lon_n), lax.rem(lon + lon_n - 1, lon_n)
    has_up, has_down = lat < lat_n - 1, lat > 0
    barrier = pltpu.get_barrier_semaphore()
    for side in (left, right):
        pl.semaphore_signal(barrier, inc=1, device_id=(lat, side), device_id_type=MESH)

    @pl.when(has_up)
    def _():
        pl.semaphore_signal(barrier, inc=1, device_id=(lat + 1, lon), device_id_type=MESH)

    @pl.when(has_down)
    def _():
        pl.semaphore_signal(barrier, inc=1, device_id=(lat - 1, lon), device_id_type=MESH)

    pl.semaphore_wait(barrier, 2 + has_up.astype(jnp.int32) + has_down.astype(jnp.int32))
    go_right = peer_copy(last_col, west, send.at[0], recv.at[0], lat, right)
    go_left = peer_copy(first_col, east, send.at[1], recv.at[1], lat, left)
    go_up = peer_copy(last_row, south, send.at[2], recv.at[2], lat + 1, lon)
    go_down = peer_copy(first_row, north, send.at[3], recv.at[3], lat - 1, lon)
    go_right.start()
    go_left.start()

    @pl.when(has_up)
    def _():
        go_up.start()

    @pl.when(has_down)
    def _():
        go_down.start()

    @pl.when(has_up)
    def _():
        go_up.wait_send()
        go_down.wait_recv()

    @pl.when(jnp.logical_not(has_up))
    def _():
        north[...] = jnp.zeros_like(north)

    @pl.when(has_down)
    def _():
        go_down.wait_send()
        go_up.wait_recv()

    @pl.when(jnp.logical_not(has_down))
    def _():
        south[...] = jnp.zeros_like(south)

    go_right.wait()
    go_left.wait()


def edge_exchange(mesh_sizes, field):
    lat_n, lon_n = mesh_sizes
    levels, rows, cols = field.shape
    row_shape = jax.ShapeDtypeStruct((levels, cols), jnp.float32)
    col_shape = jax.ShapeDtypeStruct((levels, rows), jnp.float32)
    return pl.pallas_call(
        functools.partial(edges_kernel, lat_n, lon_n),
        out_shape=[row_shape, row_shape, col_shape, col_shape],
        in_specs=[VMEM] * 4,
        out_specs=[VMEM] * 4,
        scratch_shapes=[pltpu.SemaphoreType.DMA((4,)), pltpu.SemaphoreType.DMA((4,))],
        compiler_params=params(0),
        name="edges",
    )(field[:, -1], field[:, 0], field[:, :, -1], field[:, :, 0])


def atmos_step(mesh_sizes, tracer_now, wind_u, wind_v):
    south, north, west, east = edge_exchange(mesh_sizes, tracer_now)
    east_side = jnp.concatenate([tracer_now[:, :, 1:], east[:, :, None]], axis=2)
    west_side = jnp.concatenate([west[:, :, None], tracer_now[:, :, :-1]], axis=2)
    north_side = jnp.concatenate([tracer_now[:, 1:], north[:, None]], axis=1)
    south_side = jnp.concatenate([south[:, None], tracer_now[:, :-1]], axis=1)
    advect = wind_u * (east_side - west_side) + wind_v * (north_side - south_side)
    spread_sum = east_side + west_side + north_side + south_side - 4.0 * tracer_now
    return tracer_now - advect_coef * advect + diffuse_coef * spread_sum


def dot3(x, high, low, contract):
    x_high = x.astype(jnp.bfloat16)
    x_low = (x - x_high.astype(jnp.float32)).astype(jnp.bfloat16)

    def one(a, b):
        return lax.dot_general(
            a, b, (((1,), (contract,)), ((), ())), preferred_element_type=jnp.float32
        )

    return one(x_low, high) + one(x_high, low) + one(x_high, high)


def filter_kernel(lat_n, band, chunks, q, w, h0, l0, h2, l2, h1, l1, out,
                  rx, tx, send, recv, back_send, back_recv):
    lat, lon = lax.axis_index("lat"), lax.axis_index("lon")
    levels, rows, cols = q.shape
    each = levels // 4
    part = each // chunks
    polar = jnp.logical_or(lat < band, lat >= lat_n - band)

    @pl.when(jnp.logical_not(polar))
    def _():
        out[...] = q[...]

    @pl.when(polar)
    def _():
        barrier = pltpu.get_barrier_semaphore()
        for d in (1, 2, 3):
            pl.semaphore_signal(
                barrier, inc=1, device_id=(lat, lax.rem(lon + d, 4)), device_id_type=MESH
            )
        pl.semaphore_wait(barrier, 3)
        there, home = [], []
        for c in range(chunks):
            for d in (2, 3, 1):
                dest = lax.rem(lon + d, 4)
                copy = peer_copy(
                    q.at[pl.ds(dest * each + c * part, part)],
                    rx.at[lon, pl.ds(c * part, part)],
                    send.at[c, d - 1], recv.at[c, d - 1], lat, dest,
                )
                copy.start()
                there.append(copy)
        rx[pl.ds(lon, 1)] = q[pl.ds(lon * each, each)][None]
        for c in range(chunks):
            for copy in there[3 * c:3 * c + 3]:
                copy.wait_recv()
            lines = part * rows
            x = [rx[j, c * part:(c + 1) * part].reshape(lines, cols) for j in range(4)]
            even, odd = x[0] + x[2], x[1] + x[3]
            a, b = x[0] - x[2], x[1] - x[3]

            def weigh(coeffs, start):
                width = coeffs.shape[1]
                scaled = coeffs.reshape(part, rows, width) * w[:, start:start + width][None]
                return scaled.reshape(lines, width)

            f0 = weigh(dot3(even + odd, h0[...], l0[...], 0), 0)
            f2 = weigh(dot3(even - odd, h2[...], l2[...], 0), cols)
            f1 = dot3(a, h1[:cols], l1[:cols], 0) + dot3(b, h1[cols:], l1[cols:], 0)
            f1 = weigh(f1, 2 * cols)
            y0 = dot3(f0, h0[...], l0[...], 1)
            y2 = dot3(f2, h2[...], l2[...], 1)
            a = dot3(f1, h1[:cols], l1[:cols], 1)
            b = dot3(f1, h1[cols:], l1[cols:], 1)
            plus, minus = y0 + y2, y0 - y2
            for j, y in enumerate((plus + a, minus + b, plus - a, minus - b)):
                tx[j, c * part:(c + 1) * part] = y.reshape(part, rows, cols)
            for d in (2, 3, 1):
                dest = lax.rem(lon + d, 4)
                copy = peer_copy(
                    tx.at[dest, pl.ds(c * part, part)],
                    out.at[pl.ds(lon * each + c * part, part)],
                    back_send.at[c, d - 1], back_recv.at[c, d - 1], lat, dest,
                )
                copy.start()
                home.append(copy)
        out[pl.ds(lon * each, each)] = tx[pl.ds(lon, 1)][0]
        for copy in there:
            copy.wait_send()
        for d_at, copy in enumerate(home):
            copy.wait()


def polar_filter(lat_n, band, q, weights, bases):
    levels, rows, cols = q.shape
    chunks = 2
    each = levels // 4
    sems = [pltpu.SemaphoreType.DMA((chunks, 3))] * 4
    return pl.pallas_call(
        functools.partial(filter_kernel, lat_n, band, chunks),
        out_shape=jax.ShapeDtypeStruct(q.shape, jnp.float32),
        in_specs=[VMEM] * 8,
        out_specs=VMEM,
        scratch_shapes=[pltpu.VMEM((4, each, rows, cols), jnp.float32)] * 2 + sems,
        compiler_params=params(1),
        name="polar_filter",
    )(q, weights, *bases)


AROUND = [(dy, dx) for dy in (-1, 0, 1) for dx in (-1, 0, 1) if (dy, dx) != (0, 0)]


def around_exchange(lat_n, lon_n, pieces, send, recv, fill):
    lat, lon = lax.axis_index("lat"), lax.axis_index("lon")
    has = {0: None, 1: lat < lat_n - 1, -1: lat > 0}

    def guarded(dy, action):
        if dy == 0:
            action()
        else:
            pl.when(has[dy])(action)

    def side(dx):
        return lax.rem(lon + dx + lon_n, lon_n)

    barrier = pltpu.get_barrier_semaphore()

    def greet(dy):
        for dx in (-1, 0, 1):
            if (dy, dx) != (0, 0):
                pl.semaphore_signal(
                    barrier, inc=1, device_id=(lat + dy, side(dx)), device_id_type=MESH
                )

    for dy in (0, 1, -1):
        guarded(dy, functools.partial(greet, dy))
    fill(has)
    pl.semaphore_wait(barrier, 2 + 3 * (has[1].astype(jnp.int32) + has[-1].astype(jnp.int32)))
    copies = {}
    for at, (dy, dx) in enumerate(AROUND):
        src, dst = pieces(dy, dx)
        copies[dy, dx] = peer_copy(src, dst, send.at[at], recv.at[at], lat + dy, side(dx))
    for dy in (0, 1, -1):
        group = [copies[dy, dx] for dx in (-1, 0, 1) if (dy, dx) != (0, 0)]

        def begin(group=group):
            for copy in group:
                copy.start()

        guarded(dy, begin)
    for dy in (0, 1, -1):
        group = [copies[dy, dx] for dx in (-1, 0, 1) if (dy, dx) != (0, 0)]
        other = [copies[-dy, dx] for dx in (-1, 0, 1) if (dy, dx) != (0, 0)]

        def end(group=group, other=other):
            for copy in group:
                copy.wait_send()
            for copy in other:
                copy.wait_recv()

        guarded(dy, end)


def rim_kernel(lat_n, lon_n, bottom, got, send, recv):
    at = {piece: index for index, piece in enumerate(AROUND)}
    around_exchange(
        lat_n, lon_n, lambda dy, dx: (bottom, got.at[at[dy, dx]]), send, recv, lambda has: None
    )


def rim_exchange(lat_n, lon_n, bottom):
    return pl.pallas_call(
        functools.partial(rim_kernel, lat_n, lon_n),
        out_shape=jax.ShapeDtypeStruct((8,) + bottom.shape, jnp.float32),
        in_specs=[VMEM],
        out_specs=VMEM,
        scratch_shapes=[pltpu.SemaphoreType.DMA((8,)), pltpu.SemaphoreType.DMA((8,))],
        compiler_params=params(2),
        name="rim",
    )(bottom)


def remap_kernel(table, row, col, out):
    fields, table_rows, width = table.shape
    blocks = width // 128
    column_blocks = row.shape[1] // 128

    def one(step, carry):
        i = pl.multiple_of(step // column_blocks * 8, 8)
        j = pl.multiple_of(step % column_blocks * 128, 128)
        r = row[pl.ds(i, 8), pl.ds(j, 128)]
        c = col[pl.ds(i, 8), pl.ds(j, 128)]
        key = r * blocks + c // 128
        lane = c % 128
        totals = [jnp.zeros((8, 128), jnp.float32)] * fields
        for tr in range(table_rows):
            for tb in range(blocks):
                hit = key == tr * blocks + tb
                for f in range(fields):
                    line = table[f, tr:tr + 1, tb * 128:(tb + 1) * 128]
                    wide = jnp.broadcast_to(line, (8, 128))
                    got = jnp.take_along_axis(wide, lane, axis=1, mode="promise_in_bounds")
                    totals[f] = jnp.where(hit, got, totals[f])
        for f in range(fields):
            out[f, pl.ds(i, 8), pl.ds(j, 128)] = totals[f]
        return carry

    lax.fori_loop(0, row.shape[0] // 8 * column_blocks, one, 0)


def remap(table, row, col):
    return pl.pallas_call(
        remap_kernel,
        out_shape=jax.ShapeDtypeStruct((table.shape[0],) + row.shape, jnp.float32),
        in_specs=[VMEM] * 3,
        out_specs=VMEM,
        compiler_params=params(),
        name="remap",
    )(table, row, col)


def ocean_kernel(lat_n, lon_n, temp, mask, air, out, ext, send, recv):
    level_count, rows, cols = temp.shape
    high, wide = rows + 16, cols + 256

    def fill(has):
        ext[0:level_count, 8:8 + rows, 128:128 + cols] = temp[...]
        ext[level_count, 8:8 + rows, 128:128 + cols] = mask[...].astype(jnp.float32)
        ext[level_count + 1:level_count + 3, 8:8 + rows, 128:128 + cols] = air[...]

        @pl.when(jnp.logical_not(has[1]))
        def _():
            ext[:, 8 + rows:, :] = jnp.zeros((level_count + 3, 8, wide), jnp.float32)

        @pl.when(jnp.logical_not(has[-1]))
        def _():
            ext[:, :8, :] = jnp.zeros((level_count + 3, 8, wide), jnp.float32)

    source_rows = {-1: (8, 8), 0: (8, rows), 1: (rows, 8)}
    target_rows = {-1: (8 + rows, 8), 0: (8, rows), 1: (0, 8)}
    source_cols = {-1: (128, 128), 0: (128, cols), 1: (cols, 128)}
    target_cols = {-1: (128 + cols, 128), 0: (128, cols), 1: (0, 128)}

    def pieces(dy, dx):
        def view(r, c):
            return ext.at[:, pl.ds(*r), pl.ds(*c)]

        return (
            view(source_rows[dy], source_cols[dx]),
            view(target_rows[dy], target_cols[dx]),
        )

    around_exchange(lat_n, lon_n, pieces, send, recv, fill)
    sea = ext[level_count]
    air_temp = ext[level_count + 1]
    gain = sea * flux_coef * ext[level_count + 2]

    def shifts(x):
        return (
            pltpu.roll(x, wide - 1, 1), pltpu.roll(x, 1, 1),
            pltpu.roll(x, high - 1, 0), pltpu.roll(x, 1, 0),
        )

    couplings = [ocean_diffuse * sea * s for s in shifts(sea)]
    total = couplings[0] + couplings[1] + couplings[2] + couplings[3]
    mix = vertical_mix * sea
    levels = [ext[l] for l in range(level_count)]
    for _ in range(OSTEPS):
        levels[0] = levels[0] + gain * (air_temp - levels[0])
        for l in range(level_count):
            t = levels[l]
            moved = shifts(t)
            flow = couplings[0] * (moved[0] - t)
            for k in range(1, 4):
                flow = flow + couplings[k] * (moved[k] - t)
            levels[l] = t + flow
        upper = [levels[0]] + levels[:-1]
        lower = levels[1:] + [levels[-1]]
        levels = [
            t + mix * (u + d - 2.0 * t) for t, u, d in zip(levels, upper, lower)
        ]
    for l in range(level_count):
        out[l] = levels[l][8:8 + rows, 128:128 + cols]


def ocean(lat_n, lon_n, temp, mask, air):
    level_count, rows, cols = temp.shape
    return pl.pallas_call(
        functools.partial(ocean_kernel, lat_n, lon_n),
        out_shape=jax.ShapeDtypeStruct(temp.shape, jnp.float32),
        in_specs=[VMEM] * 3,
        out_specs=VMEM,
        scratch_shapes=[
            pltpu.VMEM((level_count + 3, rows + 16, cols + 256), jnp.float32),
            pltpu.SemaphoreType.DMA((8,)),
            pltpu.SemaphoreType.DMA((8,)),
        ],
        compiler_params=params(3),
        name="ocean",
    )(temp, mask, air)


def rim_table(bottom, around, lat_place, lat_n):
    got = {piece: around[index] for index, piece in enumerate(AROUND)}
    north_row = jnp.concatenate(
        [got[-1, 1][:, :1, -1:], got[-1, 0][:, :1], got[-1, -1][:, :1, :1]], axis=2
    )
    south_row = jnp.concatenate(
        [got[1, 1][:, -1:, -1:], got[1, 0][:, -1:], got[1, -1][:, -1:, :1]], axis=2
    )
    middle = jnp.concatenate([got[0, 1][:, :, -1:], bottom, got[0, -1][:, :, :1]], axis=2)
    table = jnp.concatenate([south_row, middle, north_row], axis=1)
    width = table.shape[2]
    return jnp.pad(table, ((0, 0), (0, 0), (0, -width % 128)))


def per_device(tracer, wind_u, wind_v, ocean_temp, land_mask, remap_rows, remap_cols, polar_rows):
    levels, row_count, lon_local = tracer.shape
    lat_devices = lax.axis_size("lat")
    lon_devices = lax.axis_size("lon")
    sizes = (lat_devices, lon_devices)
    lat_total = row_count * lat_devices
    lon_total = lon_local * lon_devices
    band_devices = lat_devices // 8
    band_rows = band_devices * row_count
    lat_place = lax.axis_index("lat")
    lon_place = lax.axis_index("lon")
    matrices, waves, scale = make_bases(lon_total)
    bases = []
    for matrix in matrices:
        bases.extend(jnp.asarray(part) for part in split_basis(matrix))
    own_rows = lat_place * row_count + jnp.arange(row_count, dtype=jnp.int32)
    weights = (
        damp_table(own_rows, polar_rows, jnp.asarray(waves), lat_total, band_rows, lon_total)
        * jnp.asarray(scale)[None, :]
    )
    tracer_now = tracer
    for _ in range(STEPS):
        tracer_now = atmos_step(sizes, tracer_now, wind_u, wind_v)
        tracer_now = polar_filter(lat_devices, band_devices, tracer_now, weights, bases)
    bottom = jnp.stack(
        [tracer_now[levels - 1], jnp.abs(wind_u[levels - 1]) + jnp.abs(wind_v[levels - 1]) + 0.5]
    )
    around = rim_exchange(lat_devices, lon_devices, bottom)
    table = rim_table(bottom, around, lat_place, lat_devices)
    local_row = remap_rows - lat_place * row_count + 1
    local_col = (remap_cols - lon_place * lon_local + 1) % lon_total
    air = remap(table, local_row, local_col)
    return (tracer_now, ocean(lat_devices, lon_devices, ocean_temp, land_mask, air))


def solution(mesh):
    in_specs = (
        P(None, "lat", "lon"),
        P(None, "lat", "lon"),
        P(None, "lat", "lon"),
        P(None, "lat", "lon"),
        P("lat", "lon"),
        P("lat", "lon"),
        P("lat", "lon"),
        P(),
    )
    out_specs = (P(None, "lat", "lon"), P(None, "lat", "lon"))
    return jax.shard_map(
        per_device, mesh=mesh, in_specs=in_specs, out_specs=out_specs, check_vma=False
    )
```

```python
import functools
import math

import jax
import jax.numpy as jnp
import ml_dtypes
import numpy as np
from jax import lax
from jax.experimental import pallas as pl
from jax.experimental.pallas import tpu as pltpu
from jax.sharding import PartitionSpec as P

STEPS = 2
OSTEPS = 2
MESH = pl.DeviceIdType.MESH
VMEM = pl.BlockSpec(memory_space=pltpu.VMEM)

advect_coef = 0.2
diffuse_coef = 0.1
flux_coef = 0.25
ocean_diffuse = 0.15
vertical_mix = 0.2


def params(cid=None):
    if cid is None:
        return pltpu.CompilerParams(vmem_limit_bytes=48 * 2**20)
    return pltpu.CompilerParams(
        collective_id=cid, has_side_effects=True, vmem_limit_bytes=48 * 2**20
    )


def split_basis(matrix):
    high = matrix.astype(ml_dtypes.bfloat16)
    low = (matrix - high.astype(np.float64)).astype(ml_dtypes.bfloat16)
    return high, low


def make_bases(lon_total):
    quarter = lon_total // 4
    n = np.arange(quarter)[:, None]

    def angle(k):
        return 2.0 * math.pi * ((n * k[None, :]) % lon_total) / lon_total

    k0 = 4 * np.arange(quarter // 2 + 1)
    k0s = 4 * np.arange(1, quarter // 2)
    m0 = np.concatenate([np.cos(angle(k0)), np.sin(angle(k0s))], axis=1)
    kk0 = np.concatenate([k0, k0s])
    s0 = np.where((kk0 == 0) | (kk0 == lon_total // 2), 1.0 / quarter, 2.0 / quarter)
    k2 = 4 * np.arange(quarter // 2) + 2
    m2 = np.concatenate([np.cos(angle(k2)), np.sin(angle(k2))], axis=1)
    kk2 = np.concatenate([k2, k2])
    s2 = np.full(quarter, 2.0 / quarter)
    k1 = 4 * np.arange(quarter) + 1
    cos1, sin1 = np.cos(angle(k1)), np.sin(angle(k1))
    m1 = np.concatenate(
        [np.concatenate([cos1, -sin1], axis=1), np.concatenate([-sin1, -cos1], axis=1)], axis=0
    )
    f1 = np.minimum(k1, lon_total - k1)
    kk1 = np.concatenate([f1, f1])
    s1 = np.full(2 * quarter, 1.0 / quarter)
    waves = np.concatenate([kk0, kk2, kk1]).astype(np.float32)
    scale = np.concatenate([s0 / 4, s2 / 4, s1 / 2]).astype(np.float32)
    return (m0, m2, m1), waves, scale


def damp_table(row_index, polar_rows, wave_numbers, lat_total, band_rows, lon_total):
    latitude_cos = jnp.sin(math.pi * (row_index.astype(jnp.float32) + 0.5) / lat_total)
    ratio = latitude_cos / math.sin(math.pi * band_rows / lat_total)
    wave_sine = jnp.sin(math.pi * wave_numbers / lon_total)
    safe_sine = jnp.where(wave_numbers > 0.5, wave_sine, 1.0)
    damping = jnp.where(
        wave_numbers[None, :] > 0.5, jnp.minimum(1.0, ratio[:, None] / safe_sine[None, :]), 1.0
    )
    listed = jnp.any(row_index[:, None] == polar_rows[None, :], axis=1)
    return jnp.where(listed[:, None], damping, 1.0)


def peer_copy(src, dst, send_sem, recv_sem, lat, lon):
    return pltpu.make_async_remote_copy(
        src_ref=src, dst_ref=dst, send_sem=send_sem, recv_sem=recv_sem,
        device_id=(lat, lon), device_id_type=MESH,
    )


def edges_kernel(lat_n, lon_n, last_row, first_row, last_col, first_col,
                 south, north, west, east, send, recv):
    lat, lon = lax.axis_index("lat"), lax.axis_index("lon")
    right, left = lax.rem(lon + 1, lon_n), lax.rem(lon + lon_n - 1, lon_n)
    has_up, has_down = lat < lat_n - 1, lat > 0
    barrier = pltpu.get_barrier_semaphore()
    for side in (left, right):
        pl.semaphore_signal(barrier, inc=1, device_id=(lat, side), device_id_type=MESH)

    @pl.when(has_up)
    def _():
        pl.semaphore_signal(barrier, inc=1, device_id=(lat + 1, lon), device_id_type=MESH)

    @pl.when(has_down)
    def _():
        pl.semaphore_signal(barrier, inc=1, device_id=(lat - 1, lon), device_id_type=MESH)

    pl.semaphore_wait(barrier, 2 + has_up.astype(jnp.int32) + has_down.astype(jnp.int32))
    go_right = peer_copy(last_col, west, send.at[0], recv.at[0], lat, right)
    go_left = peer_copy(first_col, east, send.at[1], recv.at[1], lat, left)
    go_up = peer_copy(last_row, south, send.at[2], recv.at[2], lat + 1, lon)
    go_down = peer_copy(first_row, north, send.at[3], recv.at[3], lat - 1, lon)
    go_right.start()
    go_left.start()

    @pl.when(has_up)
    def _():
        go_up.start()

    @pl.when(has_down)
    def _():
        go_down.start()

    @pl.when(has_up)
    def _():
        go_up.wait_send()
        go_down.wait_recv()

    @pl.when(jnp.logical_not(has_up))
    def _():
        north[...] = jnp.zeros_like(north)

    @pl.when(has_down)
    def _():
        go_down.wait_send()
        go_up.wait_recv()

    @pl.when(jnp.logical_not(has_down))
    def _():
        south[...] = jnp.zeros_like(south)

    go_right.wait()
    go_left.wait()


def edge_exchange(mesh_sizes, field):
    lat_n, lon_n = mesh_sizes
    levels, rows, cols = field.shape
    row_shape = jax.ShapeDtypeStruct((levels, cols), jnp.float32)
    col_shape = jax.ShapeDtypeStruct((levels, rows), jnp.float32)
    return pl.pallas_call(
        functools.partial(edges_kernel, lat_n, lon_n),
        out_shape=[row_shape, row_shape, col_shape, col_shape],
        in_specs=[VMEM] * 4,
        out_specs=[VMEM] * 4,
        scratch_shapes=[pltpu.SemaphoreType.DMA((4,)), pltpu.SemaphoreType.DMA((4,))],
        compiler_params=params(0),
        name="edges",
    )(field[:, -1], field[:, 0], field[:, :, -1], field[:, :, 0])


def atmos_step(mesh_sizes, tracer_now, wind_u, wind_v):
    south, north, west, east = edge_exchange(mesh_sizes, tracer_now)
    east_side = jnp.concatenate([tracer_now[:, :, 1:], east[:, :, None]], axis=2)
    west_side = jnp.concatenate([west[:, :, None], tracer_now[:, :, :-1]], axis=2)
    north_side = jnp.concatenate([tracer_now[:, 1:], north[:, None]], axis=1)
    south_side = jnp.concatenate([south[:, None], tracer_now[:, :-1]], axis=1)
    advect = wind_u * (east_side - west_side) + wind_v * (north_side - south_side)
    spread_sum = east_side + west_side + north_side + south_side - 4.0 * tracer_now
    return tracer_now - advect_coef * advect + diffuse_coef * spread_sum


def dot3(x, high, low, contract):
    lines = x.shape[0]
    x_high = x.astype(jnp.bfloat16)
    x_low = (x - x_high.astype(jnp.float32)).astype(jnp.bfloat16)

    def one(a, b):
        return lax.dot_general(
            a, b, (((1,), (contract,)), ((), ())), preferred_element_type=jnp.float32
        )

    both = one(jnp.concatenate([x_high, x_low], axis=0), high)
    return (both[lines:] + one(x_high, low)) + both[:lines]


def filter_kernel(lat_n, band, slots, row_of, slot_of, listed, q, w, h0, l0, h2, l2, h1, l1, out,
                  packed, got, rx, tx, send, recv, back_send, back_recv):
    lat, lon = lax.axis_index("lat"), lax.axis_index("lon")
    levels, rows, cols = q.shape
    each = levels // 4
    lines = each * slots
    polar = jnp.logical_or(lat < band, lat >= lat_n - band)

    @pl.when(jnp.logical_not(polar))
    def _():
        out[...] = q[...]

    @pl.when(polar)
    def _():
        barrier = pltpu.get_barrier_semaphore()
        for d in (1, 2, 3):
            pl.semaphore_signal(
                barrier, inc=1, device_id=(lat, lax.rem(lon + d, 4)), device_id_type=MESH
            )
        for s in range(slots):
            packed[:, s:s + 1, :] = q[:, pl.ds(row_of[s], 1), :]
        pl.semaphore_wait(barrier, 3)
        there, home = [], []
        for d in (2, 3, 1):
            dest = lax.rem(lon + d, 4)
            copy = peer_copy(
                packed.at[pl.ds(dest * each, each)], rx.at[lon],
                send.at[d - 1], recv.at[d - 1], lat, dest,
            )
            copy.start()
            there.append(copy)
        rx[pl.ds(lon, 1)] = packed[pl.ds(lon * each, each)][None]
        for copy in there:
            copy.wait_recv()
        x = [rx[j].reshape(lines, cols) for j in range(4)]
        even, odd = x[0] + x[2], x[1] + x[3]
        a, b = x[0] - x[2], x[1] - x[3]

        def weigh(coeffs, start):
            width = coeffs.shape[1]
            scaled = coeffs.reshape(each, slots, width) * w[:, start:start + width][None]
            return scaled.reshape(lines, width)

        f0 = weigh(dot3(even + odd, h0[...], l0[...], 0), 0)
        f2 = weigh(dot3(even - odd, h2[...], l2[...], 0), cols)
        f1 = dot3(a, h1[:cols], l1[:cols], 0) + dot3(b, h1[cols:], l1[cols:], 0)
        f1 = weigh(f1, 2 * cols)
        y0 = dot3(f0, h0[...], l0[...], 1)
        y2 = dot3(f2, h2[...], l2[...], 1)
        a = dot3(f1, h1[:cols], l1[:cols], 1)
        b = dot3(f1, h1[cols:], l1[cols:], 1)
        plus, minus = y0 + y2, y0 - y2
        for j, y in enumerate((plus + a, minus + b, plus - a, minus - b)):
            tx[j] = y.reshape(each, slots, cols)
        for d in (2, 3, 1):
            dest = lax.rem(lon + d, 4)
            copy = peer_copy(
                tx.at[dest], got.at[pl.ds(lon * each, each)],
                back_send.at[d - 1], back_recv.at[d - 1], lat, dest,
            )
            copy.start()
            home.append(copy)
        got[pl.ds(lon * each, each)] = tx[pl.ds(lon, 1)][0]
        for copy in there:
            copy.wait_send()
        for copy in home:
            copy.wait()
        for r in range(rows):
            kept = q[:, r:r + 1, :]
            filtered = got[:, pl.ds(slot_of[r], 1), :]
            out[:, r:r + 1, :] = jnp.where(listed[r] > 0, filtered, kept)


def polar_filter(lat_n, band, slots, cid, q, plan, bases):
    levels, rows, cols = q.shape
    each = levels // 4
    smem = pl.BlockSpec(memory_space=pltpu.SMEM)
    sems = [pltpu.SemaphoreType.DMA((3,))] * 4
    whole = pltpu.VMEM((levels, slots, cols), jnp.float32)
    parts = pltpu.VMEM((4, each, slots, cols), jnp.float32)
    row_of, slot_of, listed, weights = plan
    return pl.pallas_call(
        functools.partial(filter_kernel, lat_n, band, slots),
        out_shape=jax.ShapeDtypeStruct(q.shape, jnp.float32),
        in_specs=[smem] * 3 + [VMEM] * 8,
        out_specs=VMEM,
        scratch_shapes=[whole, whole, parts, parts] + sems,
        compiler_params=params(cid),
        name="polar_filter",
    )(row_of, slot_of, listed, q, weights, *bases)


AROUND = [(dy, dx) for dy in (-1, 0, 1) for dx in (-1, 0, 1) if (dy, dx) != (0, 0)]


def around_exchange(lat_n, lon_n, pieces, send, recv, fill):
    lat, lon = lax.axis_index("lat"), lax.axis_index("lon")
    has = {0: None, 1: lat < lat_n - 1, -1: lat > 0}

    def guarded(dy, action):
        if dy == 0:
            action()
        else:
            pl.when(has[dy])(action)

    def side(dx):
        return lax.rem(lon + dx + lon_n, lon_n)

    barrier = pltpu.get_barrier_semaphore()

    def greet(dy):
        for dx in (-1, 0, 1):
            if (dy, dx) != (0, 0):
                pl.semaphore_signal(
                    barrier, inc=1, device_id=(lat + dy, side(dx)), device_id_type=MESH
                )

    for dy in (0, 1, -1):
        guarded(dy, functools.partial(greet, dy))
    fill(has)
    pl.semaphore_wait(barrier, 2 + 3 * (has[1].astype(jnp.int32) + has[-1].astype(jnp.int32)))
    copies = {}
    for at, (dy, dx) in enumerate(AROUND):
        src, dst = pieces(dy, dx)
        copies[dy, dx] = peer_copy(src, dst, send.at[at], recv.at[at], lat + dy, side(dx))
    for dy in (0, 1, -1):
        group = [copies[dy, dx] for dx in (-1, 0, 1) if (dy, dx) != (0, 0)]

        def begin(group=group):
            for copy in group:
                copy.start()

        guarded(dy, begin)
    for dy in (0, 1, -1):
        group = [copies[dy, dx] for dx in (-1, 0, 1) if (dy, dx) != (0, 0)]
        other = [copies[-dy, dx] for dx in (-1, 0, 1) if (dy, dx) != (0, 0)]

        def end(group=group, other=other):
            for copy in group:
                copy.wait_send()
            for copy in other:
                copy.wait_recv()

        guarded(dy, end)


def rim_kernel(lat_n, lon_n, bottom, got, send, recv):
    at = {piece: index for index, piece in enumerate(AROUND)}
    rows = bottom.shape[1]
    start = {-1: 0, 0: 0, 1: rows - 8}

    def pieces(dy, dx):
        span = pl.ds(start[dy], rows if dy == 0 else 8)
        return bottom.at[:, span], got.at[at[dy, dx], :, span]

    around_exchange(lat_n, lon_n, pieces, send, recv, lambda has: None)


def rim_exchange(lat_n, lon_n, bottom):
    return pl.pallas_call(
        functools.partial(rim_kernel, lat_n, lon_n),
        out_shape=jax.ShapeDtypeStruct((8,) + bottom.shape, jnp.float32),
        in_specs=[VMEM],
        out_specs=VMEM,
        scratch_shapes=[pltpu.SemaphoreType.DMA((8,)), pltpu.SemaphoreType.DMA((8,))],
        compiler_params=params(2),
        name="rim",
    )(bottom)


def remap_kernel(table, row, col, out):
    fields, table_rows, width = table.shape
    blocks = width // 128
    column_blocks = row.shape[1] // 128

    def one(step, carry):
        i = pl.multiple_of(step // column_blocks * 8, 8)
        j = pl.multiple_of(step % column_blocks * 128, 128)
        r = row[pl.ds(i, 8), pl.ds(j, 128)]
        c = col[pl.ds(i, 8), pl.ds(j, 128)]
        key = r * blocks + c // 128
        lane = c % 128
        totals = [jnp.zeros((8, 128), jnp.float32)] * fields
        for tr in range(table_rows):
            for tb in range(blocks):
                hit = key == tr * blocks + tb
                for f in range(fields):
                    line = table[f, tr:tr + 1, tb * 128:(tb + 1) * 128]
                    wide = jnp.broadcast_to(line, (8, 128))
                    got = jnp.take_along_axis(wide, lane, axis=1, mode="promise_in_bounds")
                    totals[f] = jnp.where(hit, got, totals[f])
        for f in range(fields):
            out[f, pl.ds(i, 8), pl.ds(j, 128)] = totals[f]
        return carry

    lax.fori_loop(0, row.shape[0] // 8 * column_blocks, one, 0)


def remap(table, row, col):
    return pl.pallas_call(
        remap_kernel,
        out_shape=jax.ShapeDtypeStruct((table.shape[0],) + row.shape, jnp.float32),
        in_specs=[VMEM] * 3,
        out_specs=VMEM,
        compiler_params=params(),
        name="remap",
    )(table, row, col)


def ocean_kernel(lat_n, lon_n, temp, mask, air, out, ext, send, recv):
    level_count, rows, cols = temp.shape
    high, wide = rows + 16, cols + 256

    def fill(has):
        ext[0:level_count, 8:8 + rows, 128:128 + cols] = temp[...]
        ext[level_count, 8:8 + rows, 128:128 + cols] = mask[...].astype(jnp.float32)
        ext[level_count + 1:level_count + 3, 8:8 + rows, 128:128 + cols] = air[...]

        @pl.when(jnp.logical_not(has[1]))
        def _():
            ext[:, 8 + rows:, :] = jnp.zeros((level_count + 3, 8, wide), jnp.float32)

        @pl.when(jnp.logical_not(has[-1]))
        def _():
            ext[:, :8, :] = jnp.zeros((level_count + 3, 8, wide), jnp.float32)

    source_rows = {-1: (8, 8), 0: (8, rows), 1: (rows, 8)}
    target_rows = {-1: (8 + rows, 8), 0: (8, rows), 1: (0, 8)}
    source_cols = {-1: (128, 128), 0: (128, cols), 1: (cols, 128)}
    target_cols = {-1: (128 + cols, 128), 0: (128, cols), 1: (0, 128)}

    def pieces(dy, dx):
        def view(r, c):
            return ext.at[:, pl.ds(*r), pl.ds(*c)]

        return (
            view(source_rows[dy], source_cols[dx]),
            view(target_rows[dy], target_cols[dx]),
        )

    around_exchange(lat_n, lon_n, pieces, send, recv, fill)
    sea = ext[level_count]
    air_temp = ext[level_count + 1]
    gain = sea * flux_coef * ext[level_count + 2]

    def shifts(x):
        return (
            pltpu.roll(x, wide - 1, 1), pltpu.roll(x, 1, 1),
            pltpu.roll(x, high - 1, 0), pltpu.roll(x, 1, 0),
        )

    couplings = [ocean_diffuse * sea * s for s in shifts(sea)]
    total = couplings[0] + couplings[1] + couplings[2] + couplings[3]
    mix = vertical_mix * sea
    levels = [ext[l] for l in range(level_count)]
    for _ in range(OSTEPS):
        levels[0] = levels[0] + gain * (air_temp - levels[0])
        for l in range(level_count):
            t = levels[l]
            moved = shifts(t)
            flow = couplings[0] * (moved[0] - t)
            for k in range(1, 4):
                flow = flow + couplings[k] * (moved[k] - t)
            levels[l] = t + flow
        upper = [levels[0]] + levels[:-1]
        lower = levels[1:] + [levels[-1]]
        levels = [
            t + mix * (u + d - 2.0 * t) for t, u, d in zip(levels, upper, lower)
        ]
    for l in range(level_count):
        out[l] = levels[l][8:8 + rows, 128:128 + cols]


def ocean(lat_n, lon_n, temp, mask, air):
    level_count, rows, cols = temp.shape
    return pl.pallas_call(
        functools.partial(ocean_kernel, lat_n, lon_n),
        out_shape=jax.ShapeDtypeStruct(temp.shape, jnp.float32),
        in_specs=[VMEM] * 3,
        out_specs=VMEM,
        scratch_shapes=[
            pltpu.VMEM((level_count + 3, rows + 16, cols + 256), jnp.float32),
            pltpu.SemaphoreType.DMA((8,)),
            pltpu.SemaphoreType.DMA((8,)),
        ],
        compiler_params=params(3),
        name="ocean",
    )(temp, mask, air)


def rim_table(bottom, around, lat_place, lat_n):
    got = {piece: around[index] for index, piece in enumerate(AROUND)}
    north_row = jnp.concatenate(
        [got[-1, 1][:, :1, -1:], got[-1, 0][:, :1], got[-1, -1][:, :1, :1]], axis=2
    )
    south_row = jnp.concatenate(
        [got[1, 1][:, -1:, -1:], got[1, 0][:, -1:], got[1, -1][:, -1:, :1]], axis=2
    )
    middle = jnp.concatenate([got[0, 1][:, :, -1:], bottom, got[0, -1][:, :, :1]], axis=2)
    table = jnp.concatenate([south_row, middle, north_row], axis=1)
    width = table.shape[2]
    return jnp.pad(table, ((0, 0), (0, 0), (0, -width % 128)))


def per_device(tracer, wind_u, wind_v, ocean_temp, land_mask, remap_rows, remap_cols, polar_rows):
    levels, row_count, lon_local = tracer.shape
    lat_devices = lax.axis_size("lat")
    lon_devices = lax.axis_size("lon")
    sizes = (lat_devices, lon_devices)
    lat_total = row_count * lat_devices
    lon_total = lon_local * lon_devices
    band_devices = lat_devices // 8
    band_rows = band_devices * row_count
    lat_place = lax.axis_index("lat")
    lon_place = lax.axis_index("lon")
    matrices, waves, scale = make_bases(lon_total)
    bases = []
    for matrix in matrices:
        bases.extend(jnp.asarray(part) for part in split_basis(matrix))
    band_first = lax.broadcasted_iota(jnp.int32, (lat_devices, 1), 0) * row_count
    inside = (polar_rows[None, :] >= band_first) & (polar_rows[None, :] < band_first + row_count)
    most = jnp.max(jnp.sum(inside.astype(jnp.int32), axis=1))
    local_rows = jnp.arange(row_count, dtype=jnp.int32)
    own_rows = lat_place * row_count + local_rows
    listed = jnp.any(own_rows[:, None] == polar_rows[None, :], axis=1)
    before = (local_rows[None, :] < local_rows[:, None]) & listed[None, :]
    slot_of = jnp.sum(before.astype(jnp.int32), axis=1)

    def atmosphere(slots, cid, tracer_now):
        filled = (slot_of[None, :] == jnp.arange(slots)[:, None]) & listed[None, :]
        row_of = jnp.sum(jnp.where(filled, local_rows[None, :], 0), axis=1)
        weights = (
            damp_table(
                lat_place * row_count + row_of, polar_rows, jnp.asarray(waves),
                lat_total, band_rows, lon_total,
            )
            * jnp.asarray(scale)[None, :]
        )
        plan = (row_of, jnp.minimum(slot_of, slots - 1), listed.astype(jnp.int32), weights)
        for _ in range(STEPS):
            tracer_now = atmos_step(sizes, tracer_now, wind_u, wind_v)
            tracer_now = polar_filter(
                lat_devices, band_devices, slots, cid, tracer_now, plan, bases
            )
        return tracer_now

    few = 16
    tracer_now = lax.cond(
        most <= few,
        functools.partial(atmosphere, few, 1),
        functools.partial(atmosphere, row_count, 4),
        tracer,
    )
    bottom = jnp.stack(
        [tracer_now[levels - 1], jnp.abs(wind_u[levels - 1]) + jnp.abs(wind_v[levels - 1]) + 0.5]
    )
    around = rim_exchange(lat_devices, lon_devices, bottom)
    table = rim_table(bottom, around, lat_place, lat_devices)
    local_row = remap_rows - lat_place * row_count + 1
    local_col = (remap_cols - lon_place * lon_local + 1) % lon_total
    air = remap(table, local_row, local_col)
    return (tracer_now, ocean(lat_devices, lon_devices, ocean_temp, land_mask, air))


def solution(mesh):
    in_specs = (
        P(None, "lat", "lon"),
        P(None, "lat", "lon"),
        P(None, "lat", "lon"),
        P(None, "lat", "lon"),
        P("lat", "lon"),
        P("lat", "lon"),
        P("lat", "lon"),
        P(),
    )
    out_specs = (P(None, "lat", "lon"), P(None, "lat", "lon"))
    return jax.shard_map(
        per_device, mesh=mesh, in_specs=in_specs, out_specs=out_specs, check_vma=False
    )
```

```python
import functools
import math

import jax
import jax.numpy as jnp
import ml_dtypes
import numpy as np
from jax import lax
from jax.experimental import pallas as pl
from jax.experimental.pallas import tpu as pltpu
from jax.sharding import PartitionSpec as P

STEPS = 2
OSTEPS = 2
MESH = pl.DeviceIdType.MESH
VMEM = pl.BlockSpec(memory_space=pltpu.VMEM)

advect_coef = 0.2
diffuse_coef = 0.1
flux_coef = 0.25
ocean_diffuse = 0.15
vertical_mix = 0.2


def params(cid=None):
    if cid is None:
        return pltpu.CompilerParams(vmem_limit_bytes=48 * 2**20)
    return pltpu.CompilerParams(
        collective_id=cid, has_side_effects=True, vmem_limit_bytes=48 * 2**20
    )


def split_basis(matrix):
    high = matrix.astype(ml_dtypes.bfloat16)
    low = (matrix - high.astype(np.float64)).astype(ml_dtypes.bfloat16)
    return high, low


def make_bases(lon_total):
    quarter = lon_total // 4
    n = np.arange(quarter)[:, None]

    def angle(k):
        return 2.0 * math.pi * ((n * k[None, :]) % lon_total) / lon_total

    k0 = 4 * np.arange(quarter // 2 + 1)
    k0s = 4 * np.arange(1, quarter // 2)
    m0 = np.concatenate([np.cos(angle(k0)), np.sin(angle(k0s))], axis=1)
    kk0 = np.concatenate([k0, k0s])
    s0 = np.where((kk0 == 0) | (kk0 == lon_total // 2), 1.0 / quarter, 2.0 / quarter)
    k2 = 4 * np.arange(quarter // 2) + 2
    m2 = np.concatenate([np.cos(angle(k2)), np.sin(angle(k2))], axis=1)
    kk2 = np.concatenate([k2, k2])
    s2 = np.full(quarter, 2.0 / quarter)
    k1 = 4 * np.arange(quarter) + 1
    cos1, sin1 = np.cos(angle(k1)), np.sin(angle(k1))
    m1 = np.concatenate(
        [np.concatenate([cos1, -sin1], axis=1), np.concatenate([-sin1, -cos1], axis=1)], axis=0
    )
    f1 = np.minimum(k1, lon_total - k1)
    kk1 = np.concatenate([f1, f1])
    s1 = np.full(2 * quarter, 1.0 / quarter)
    waves = np.concatenate([kk0, kk2, kk1]).astype(np.float32)
    scale = np.concatenate([s0 / 4, s2 / 4, s1 / 2]).astype(np.float32)
    return (m0, m2, m1), waves, scale


def damp_table(row_index, polar_rows, wave_numbers, lat_total, band_rows, lon_total):
    latitude_cos = jnp.sin(math.pi * (row_index.astype(jnp.float32) + 0.5) / lat_total)
    ratio = latitude_cos / math.sin(math.pi * band_rows / lat_total)
    wave_sine = jnp.sin(math.pi * wave_numbers / lon_total)
    safe_sine = jnp.where(wave_numbers > 0.5, wave_sine, 1.0)
    damping = jnp.where(
        wave_numbers[None, :] > 0.5, jnp.minimum(1.0, ratio[:, None] / safe_sine[None, :]), 1.0
    )
    listed = jnp.any(row_index[:, None] == polar_rows[None, :], axis=1)
    return jnp.where(listed[:, None], damping, 1.0)


def peer_copy(src, dst, send_sem, recv_sem, lat, lon):
    return pltpu.make_async_remote_copy(
        src_ref=src, dst_ref=dst, send_sem=send_sem, recv_sem=recv_sem,
        device_id=(lat, lon), device_id_type=MESH,
    )


def edges_kernel(lat_n, lon_n, last_row, first_row, last_col, first_col,
                 south, north, west, east, send, recv):
    lat, lon = lax.axis_index("lat"), lax.axis_index("lon")
    right, left = lax.rem(lon + 1, lon_n), lax.rem(lon + lon_n - 1, lon_n)
    has_up, has_down = lat < lat_n - 1, lat > 0
    barrier = pltpu.get_barrier_semaphore()
    for side in (left, right):
        pl.semaphore_signal(barrier, inc=1, device_id=(lat, side), device_id_type=MESH)

    @pl.when(has_up)
    def _():
        pl.semaphore_signal(barrier, inc=1, device_id=(lat + 1, lon), device_id_type=MESH)

    @pl.when(has_down)
    def _():
        pl.semaphore_signal(barrier, inc=1, device_id=(lat - 1, lon), device_id_type=MESH)

    pl.semaphore_wait(barrier, 2 + has_up.astype(jnp.int32) + has_down.astype(jnp.int32))
    go_right = peer_copy(last_col, west, send.at[0], recv.at[0], lat, right)
    go_left = peer_copy(first_col, east, send.at[1], recv.at[1], lat, left)
    go_up = peer_copy(last_row, south, send.at[2], recv.at[2], lat + 1, lon)
    go_down = peer_copy(first_row, north, send.at[3], recv.at[3], lat - 1, lon)
    go_right.start()
    go_left.start()

    @pl.when(has_up)
    def _():
        go_up.start()

    @pl.when(has_down)
    def _():
        go_down.start()

    @pl.when(has_up)
    def _():
        go_up.wait_send()
        go_down.wait_recv()

    @pl.when(jnp.logical_not(has_up))
    def _():
        north[...] = jnp.zeros_like(north)

    @pl.when(has_down)
    def _():
        go_down.wait_send()
        go_up.wait_recv()

    @pl.when(jnp.logical_not(has_down))
    def _():
        south[...] = jnp.zeros_like(south)

    go_right.wait()
    go_left.wait()


def edge_exchange(mesh_sizes, field):
    lat_n, lon_n = mesh_sizes
    levels, rows, cols = field.shape
    row_shape = jax.ShapeDtypeStruct((levels, cols), jnp.float32)
    col_shape = jax.ShapeDtypeStruct((levels, rows), jnp.float32)
    return pl.pallas_call(
        functools.partial(edges_kernel, lat_n, lon_n),
        out_shape=[row_shape, row_shape, col_shape, col_shape],
        in_specs=[VMEM] * 4,
        out_specs=[VMEM] * 4,
        scratch_shapes=[pltpu.SemaphoreType.DMA((4,)), pltpu.SemaphoreType.DMA((4,))],
        compiler_params=params(0),
        name="edges",
    )(field[:, -1], field[:, 0], field[:, :, -1], field[:, :, 0])


def atmos_step(mesh_sizes, tracer_now, wind_u, wind_v):
    south, north, west, east = edge_exchange(mesh_sizes, tracer_now)
    east_side = jnp.concatenate([tracer_now[:, :, 1:], east[:, :, None]], axis=2)
    west_side = jnp.concatenate([west[:, :, None], tracer_now[:, :, :-1]], axis=2)
    north_side = jnp.concatenate([tracer_now[:, 1:], north[:, None]], axis=1)
    south_side = jnp.concatenate([south[:, None], tracer_now[:, :-1]], axis=1)
    advect = wind_u * (east_side - west_side) + wind_v * (north_side - south_side)
    spread_sum = east_side + west_side + north_side + south_side - 4.0 * tracer_now
    return tracer_now - advect_coef * advect + diffuse_coef * spread_sum


def dot3(x, high, low, contract):
    lines = x.shape[0]
    x_high = x.astype(jnp.bfloat16)
    x_low = (x - x_high.astype(jnp.float32)).astype(jnp.bfloat16)

    def one(a, b):
        return lax.dot_general(
            a, b, (((1,), (contract,)), ((), ())), preferred_element_type=jnp.float32
        )

    both = one(jnp.concatenate([x_high, x_low], axis=0), high)
    return (both[lines:] + one(x_high, low)) + both[:lines]


def filter_kernel(lat_n, band, slots, row_of, slot_of, listed, q, w, h0, l0, h2, l2, h1, l1, out,
                  hold, go, rx, ret, back, send, recv, back_send, back_recv):
    lat, lon = lax.axis_index("lat"), lax.axis_index("lon")
    levels, rows, cols = q.shape
    each = levels // 4
    lines = each * slots
    full, rest = cols // 128, cols % 128
    per = 128 // rest
    polar = jnp.logical_or(lat < band, lat >= lat_n - band)

    def pack(message, j):
        base = j * each
        for t in range(full):
            message[j, t * each:(t + 1) * each] = hold[base:base + each, :, t * 128:(t + 1) * 128]
        for g in range(each // per):
            message[j, full * each + g] = jnp.concatenate(
                [hold[base + g * per + i, :, full * 128:] for i in range(per)], axis=1
            )

    def unpack(message, j):
        base = j * each
        for t in range(full):
            hold[base:base + each, :, t * 128:(t + 1) * 128] = message[j, t * each:(t + 1) * each]
        for g in range(each // per):
            tails = message[j, full * each + g]
            for i in range(per):
                hold[base + g * per + i, :, full * 128:] = tails[:, i * rest:(i + 1) * rest]

    @pl.when(jnp.logical_not(polar))
    def _():
        out[...] = q[...]

    @pl.when(polar)
    def _():
        barrier = pltpu.get_barrier_semaphore()
        for d in (1, 2, 3):
            pl.semaphore_signal(
                barrier, inc=1, device_id=(lat, lax.rem(lon + d, 4)), device_id_type=MESH
            )
        for s in range(slots):
            hold[:, s:s + 1, :] = q[:, pl.ds(row_of[s], 1), :]
        for j in range(4):
            pack(go, j)
        pl.semaphore_wait(barrier, 3)
        there, home = [], []
        for d in (2, 3, 1):
            dest = lax.rem(lon + d, 4)
            copy = peer_copy(
                go.at[dest], rx.at[lon],
                send.at[d - 1], recv.at[d - 1], lat, dest,
            )
            copy.start()
            there.append(copy)
        rx[pl.ds(lon, 1)] = go[pl.ds(lon, 1)]
        for copy in there:
            copy.wait_recv()
        for j in range(4):
            unpack(rx, j)
        x = [hold[j * each:(j + 1) * each].reshape(lines, cols) for j in range(4)]
        even, odd = x[0] + x[2], x[1] + x[3]
        a, b = x[0] - x[2], x[1] - x[3]

        def weigh(coeffs, start):
            width = coeffs.shape[1]
            scaled = coeffs.reshape(each, slots, width) * w[:, start:start + width][None]
            return scaled.reshape(lines, width)

        f0 = weigh(dot3(even + odd, h0[...], l0[...], 0), 0)
        f2 = weigh(dot3(even - odd, h2[...], l2[...], 0), cols)
        f1 = dot3(a, h1[:cols], l1[:cols], 0) + dot3(b, h1[cols:], l1[cols:], 0)
        f1 = weigh(f1, 2 * cols)
        y0 = dot3(f0, h0[...], l0[...], 1)
        y2 = dot3(f2, h2[...], l2[...], 1)
        a = dot3(f1, h1[:cols], l1[:cols], 1)
        b = dot3(f1, h1[cols:], l1[cols:], 1)
        plus, minus = y0 + y2, y0 - y2
        for j, y in enumerate((plus + a, minus + b, plus - a, minus - b)):
            hold[j * each:(j + 1) * each] = y.reshape(each, slots, cols)
            pack(ret, j)
        for d in (2, 3, 1):
            dest = lax.rem(lon + d, 4)
            copy = peer_copy(
                ret.at[dest], back.at[lon],
                back_send.at[d - 1], back_recv.at[d - 1], lat, dest,
            )
            copy.start()
            home.append(copy)
        back[pl.ds(lon, 1)] = ret[pl.ds(lon, 1)]
        for copy in there:
            copy.wait_send()
        for copy in home:
            copy.wait()
        for j in range(4):
            unpack(back, j)
        for r in range(rows):
            kept = q[:, r:r + 1, :]
            filtered = hold[:, pl.ds(slot_of[r], 1), :]
            out[:, r:r + 1, :] = jnp.where(listed[r] > 0, filtered, kept)


def polar_filter(lat_n, band, slots, cid, q, plan, bases):
    levels, rows, cols = q.shape
    each = levels // 4
    smem = pl.BlockSpec(memory_space=pltpu.SMEM)
    sems = [pltpu.SemaphoreType.DMA((3,))] * 4
    whole = pltpu.VMEM((levels, slots, cols), jnp.float32)
    per = 128 // (cols % 128)
    planes = cols // 128 * each + each // per
    parts = pltpu.VMEM((4, planes, slots, 128), jnp.float32)
    row_of, slot_of, listed, weights = plan
    return pl.pallas_call(
        functools.partial(filter_kernel, lat_n, band, slots),
        out_shape=jax.ShapeDtypeStruct(q.shape, jnp.float32),
        in_specs=[smem] * 3 + [VMEM] * 8,
        out_specs=VMEM,
        scratch_shapes=[whole] + [parts] * 4 + sems,
        compiler_params=params(cid),
        name="polar_filter",
    )(row_of, slot_of, listed, q, weights, *bases)


AROUND = [(dy, dx) for dy in (-1, 0, 1) for dx in (-1, 0, 1) if (dy, dx) != (0, 0)]


def around_exchange(lat_n, lon_n, pieces, send, recv, fill):
    lat, lon = lax.axis_index("lat"), lax.axis_index("lon")
    has = {0: None, 1: lat < lat_n - 1, -1: lat > 0}

    def guarded(dy, action):
        if dy == 0:
            action()
        else:
            pl.when(has[dy])(action)

    def side(dx):
        return lax.rem(lon + dx + lon_n, lon_n)

    barrier = pltpu.get_barrier_semaphore()

    def greet(dy):
        for dx in (-1, 0, 1):
            if (dy, dx) != (0, 0):
                pl.semaphore_signal(
                    barrier, inc=1, device_id=(lat + dy, side(dx)), device_id_type=MESH
                )

    for dy in (0, 1, -1):
        guarded(dy, functools.partial(greet, dy))
    fill(has)
    pl.semaphore_wait(barrier, 2 + 3 * (has[1].astype(jnp.int32) + has[-1].astype(jnp.int32)))
    copies = {}
    for at, (dy, dx) in enumerate(AROUND):
        src, dst = pieces(dy, dx)
        copies[dy, dx] = peer_copy(src, dst, send.at[at], recv.at[at], lat + dy, side(dx))
    for dy in (0, 1, -1):
        group = [copies[dy, dx] for dx in (-1, 0, 1) if (dy, dx) != (0, 0)]

        def begin(group=group):
            for copy in group:
                copy.start()

        guarded(dy, begin)
    for dy in (0, 1, -1):
        group = [copies[dy, dx] for dx in (-1, 0, 1) if (dy, dx) != (0, 0)]
        other = [copies[-dy, dx] for dx in (-1, 0, 1) if (dy, dx) != (0, 0)]

        def end(group=group, other=other):
            for copy in group:
                copy.wait_send()
            for copy in other:
                copy.wait_recv()

        guarded(dy, end)


def rim_kernel(lat_n, lon_n, bottom, got, send, recv):
    at = {piece: index for index, piece in enumerate(AROUND)}
    rows = bottom.shape[1]
    start = {-1: 0, 0: 0, 1: rows - 8}

    def pieces(dy, dx):
        span = pl.ds(start[dy], rows if dy == 0 else 8)
        return bottom.at[:, span], got.at[at[dy, dx], :, span]

    around_exchange(lat_n, lon_n, pieces, send, recv, lambda has: None)


def rim_exchange(lat_n, lon_n, bottom):
    return pl.pallas_call(
        functools.partial(rim_kernel, lat_n, lon_n),
        out_shape=jax.ShapeDtypeStruct((8,) + bottom.shape, jnp.float32),
        in_specs=[VMEM],
        out_specs=VMEM,
        scratch_shapes=[pltpu.SemaphoreType.DMA((8,)), pltpu.SemaphoreType.DMA((8,))],
        compiler_params=params(2),
        name="rim",
    )(bottom)


def remap_kernel(table, row, col, out):
    fields, table_rows, width = table.shape
    blocks = width // 128
    column_blocks = row.shape[1] // 128

    def one(step, carry):
        i = pl.multiple_of(step // column_blocks * 8, 8)
        j = pl.multiple_of(step % column_blocks * 128, 128)
        r = row[pl.ds(i, 8), pl.ds(j, 128)]
        c = col[pl.ds(i, 8), pl.ds(j, 128)]
        key = r * blocks + c // 128
        lane = c % 128
        totals = [jnp.zeros((8, 128), jnp.float32)] * fields
        for tr in range(table_rows):
            for tb in range(blocks):
                hit = key == tr * blocks + tb
                for f in range(fields):
                    line = table[f, tr:tr + 1, tb * 128:(tb + 1) * 128]
                    wide = jnp.broadcast_to(line, (8, 128))
                    got = jnp.take_along_axis(wide, lane, axis=1, mode="promise_in_bounds")
                    totals[f] = jnp.where(hit, got, totals[f])
        for f in range(fields):
            out[f, pl.ds(i, 8), pl.ds(j, 128)] = totals[f]
        return carry

    lax.fori_loop(0, row.shape[0] // 8 * column_blocks, one, 0)


def remap(table, row, col):
    return pl.pallas_call(
        remap_kernel,
        out_shape=jax.ShapeDtypeStruct((table.shape[0],) + row.shape, jnp.float32),
        in_specs=[VMEM] * 3,
        out_specs=VMEM,
        compiler_params=params(),
        name="remap",
    )(table, row, col)


def ocean_kernel(lat_n, lon_n, temp, mask, air, out, ext, send, recv):
    level_count, rows, cols = temp.shape
    high, wide = rows + 16, cols + 256

    def fill(has):
        ext[0:level_count, 8:8 + rows, 128:128 + cols] = temp[...]
        ext[level_count, 8:8 + rows, 128:128 + cols] = mask[...].astype(jnp.float32)
        ext[level_count + 1:level_count + 3, 8:8 + rows, 128:128 + cols] = air[...]

        @pl.when(jnp.logical_not(has[1]))
        def _():
            ext[:, 8 + rows:, :] = jnp.zeros((level_count + 3, 8, wide), jnp.float32)

        @pl.when(jnp.logical_not(has[-1]))
        def _():
            ext[:, :8, :] = jnp.zeros((level_count + 3, 8, wide), jnp.float32)

    source_rows = {-1: (8, 8), 0: (8, rows), 1: (rows, 8)}
    target_rows = {-1: (8 + rows, 8), 0: (8, rows), 1: (0, 8)}
    source_cols = {-1: (128, 128), 0: (128, cols), 1: (cols, 128)}
    target_cols = {-1: (128 + cols, 128), 0: (128, cols), 1: (0, 128)}

    def pieces(dy, dx):
        def view(r, c):
            return ext.at[:, pl.ds(*r), pl.ds(*c)]

        return (
            view(source_rows[dy], source_cols[dx]),
            view(target_rows[dy], target_cols[dx]),
        )

    around_exchange(lat_n, lon_n, pieces, send, recv, fill)
    sea = ext[level_count]
    air_temp = ext[level_count + 1]
    gain = sea * flux_coef * ext[level_count + 2]

    def shifts(x):
        return (
            pltpu.roll(x, wide - 1, 1), pltpu.roll(x, 1, 1),
            pltpu.roll(x, high - 1, 0), pltpu.roll(x, 1, 0),
        )

    couplings = [ocean_diffuse * sea * s for s in shifts(sea)]
    total = couplings[0] + couplings[1] + couplings[2] + couplings[3]
    mix = vertical_mix * sea
    levels = [ext[l] for l in range(level_count)]
    for _ in range(OSTEPS):
        levels[0] = levels[0] + gain * (air_temp - levels[0])
        for l in range(level_count):
            t = levels[l]
            moved = shifts(t)
            flow = couplings[0] * (moved[0] - t)
            for k in range(1, 4):
                flow = flow + couplings[k] * (moved[k] - t)
            levels[l] = t + flow
        upper = [levels[0]] + levels[:-1]
        lower = levels[1:] + [levels[-1]]
        levels = [
            t + mix * (u + d - 2.0 * t) for t, u, d in zip(levels, upper, lower)
        ]
    for l in range(level_count):
        out[l] = levels[l][8:8 + rows, 128:128 + cols]


def ocean(lat_n, lon_n, temp, mask, air):
    level_count, rows, cols = temp.shape
    return pl.pallas_call(
        functools.partial(ocean_kernel, lat_n, lon_n),
        out_shape=jax.ShapeDtypeStruct(temp.shape, jnp.float32),
        in_specs=[VMEM] * 3,
        out_specs=VMEM,
        scratch_shapes=[
            pltpu.VMEM((level_count + 3, rows + 16, cols + 256), jnp.float32),
            pltpu.SemaphoreType.DMA((8,)),
            pltpu.SemaphoreType.DMA((8,)),
        ],
        compiler_params=params(3),
        name="ocean",
    )(temp, mask, air)


def rim_table(bottom, around, lat_place, lat_n):
    got = {piece: around[index] for index, piece in enumerate(AROUND)}
    north_row = jnp.concatenate(
        [got[-1, 1][:, :1, -1:], got[-1, 0][:, :1], got[-1, -1][:, :1, :1]], axis=2
    )
    south_row = jnp.concatenate(
        [got[1, 1][:, -1:, -1:], got[1, 0][:, -1:], got[1, -1][:, -1:, :1]], axis=2
    )
    middle = jnp.concatenate([got[0, 1][:, :, -1:], bottom, got[0, -1][:, :, :1]], axis=2)
    table = jnp.concatenate([south_row, middle, north_row], axis=1)
    width = table.shape[2]
    return jnp.pad(table, ((0, 0), (0, 0), (0, -width % 128)))


def per_device(tracer, wind_u, wind_v, ocean_temp, land_mask, remap_rows, remap_cols, polar_rows):
    levels, row_count, lon_local = tracer.shape
    lat_devices = lax.axis_size("lat")
    lon_devices = lax.axis_size("lon")
    sizes = (lat_devices, lon_devices)
    lat_total = row_count * lat_devices
    lon_total = lon_local * lon_devices
    band_devices = lat_devices // 8
    band_rows = band_devices * row_count
    lat_place = lax.axis_index("lat")
    lon_place = lax.axis_index("lon")
    matrices, waves, scale = make_bases(lon_total)
    bases = []
    for matrix in matrices:
        bases.extend(jnp.asarray(part) for part in split_basis(matrix))
    band_first = lax.broadcasted_iota(jnp.int32, (lat_devices, 1), 0) * row_count
    inside = (polar_rows[None, :] >= band_first) & (polar_rows[None, :] < band_first + row_count)
    most = jnp.max(jnp.sum(inside.astype(jnp.int32), axis=1))
    local_rows = jnp.arange(row_count, dtype=jnp.int32)
    own_rows = lat_place * row_count + local_rows
    listed = jnp.any(own_rows[:, None] == polar_rows[None, :], axis=1)
    before = (local_rows[None, :] < local_rows[:, None]) & listed[None, :]
    slot_of = jnp.sum(before.astype(jnp.int32), axis=1)

    filled = (slot_of[None, :] == local_rows[:, None]) & listed[None, :]
    row_of = jnp.sum(jnp.where(filled, local_rows[None, :], 0), axis=1)
    weights = (
        damp_table(
            lat_place * row_count + row_of, polar_rows, jnp.asarray(waves),
            lat_total, band_rows, lon_total,
        )
        * jnp.asarray(scale)[None, :]
    )
    listed = listed.astype(jnp.int32)

    def atmosphere(slots, cid, tracer_now):
        plan = (row_of[:slots], jnp.minimum(slot_of, slots - 1), listed, weights[:slots])
        for step in range(STEPS):
            if step > 0:
                tracer_now = atmos_step(sizes, tracer_now, wind_u, wind_v)
            tracer_now = polar_filter(
                lat_devices, band_devices, slots, cid, tracer_now, plan, bases
            )
        return tracer_now

    few = 16
    tracer_now = lax.cond(
        most <= few,
        functools.partial(atmosphere, few, 1),
        functools.partial(atmosphere, row_count, 4),
        atmos_step(sizes, tracer, wind_u, wind_v),
    )
    bottom = jnp.stack(
        [tracer_now[levels - 1], jnp.abs(wind_u[levels - 1]) + jnp.abs(wind_v[levels - 1]) + 0.5]
    )
    around = rim_exchange(lat_devices, lon_devices, bottom)
    table = rim_table(bottom, around, lat_place, lat_devices)
    local_row = remap_rows - lat_place * row_count + 1
    local_col = (remap_cols - lon_place * lon_local + 1) % lon_total
    air = remap(table, local_row, local_col)
    return (tracer_now, ocean(lat_devices, lon_devices, ocean_temp, land_mask, air))


def solution(mesh):
    in_specs = (
        P(None, "lat", "lon"),
        P(None, "lat", "lon"),
        P(None, "lat", "lon"),
        P(None, "lat", "lon"),
        P("lat", "lon"),
        P("lat", "lon"),
        P("lat", "lon"),
        P(),
    )
    out_specs = (P(None, "lat", "lon"), P(None, "lat", "lon"))
    return jax.shard_map(
        per_device, mesh=mesh, in_specs=in_specs, out_specs=out_specs, check_vma=False
    )
```

```python
import functools
import math

import jax
import jax.numpy as jnp
import ml_dtypes
import numpy as np
from jax import lax
from jax.experimental import pallas as pl
from jax.experimental.pallas import tpu as pltpu
from jax.sharding import PartitionSpec as P

STEPS = 2
OSTEPS = 2
MESH = pl.DeviceIdType.MESH
VMEM = pl.BlockSpec(memory_space=pltpu.VMEM)

advect_coef = 0.2
diffuse_coef = 0.1
flux_coef = 0.25
ocean_diffuse = 0.15
vertical_mix = 0.2


def params(cid=None):
    if cid is None:
        return pltpu.CompilerParams(vmem_limit_bytes=48 * 2**20)
    return pltpu.CompilerParams(
        collective_id=cid, has_side_effects=True, vmem_limit_bytes=48 * 2**20
    )


def split_basis(matrix):
    high = matrix.astype(ml_dtypes.bfloat16)
    low = (matrix - high.astype(np.float64)).astype(ml_dtypes.bfloat16)
    return high, low


def make_bases(lon_total):
    quarter = lon_total // 4
    n = np.arange(quarter)[:, None]

    def angle(k):
        return 2.0 * math.pi * ((n * k[None, :]) % lon_total) / lon_total

    k0 = 4 * np.arange(quarter // 2 + 1)
    k0s = 4 * np.arange(1, quarter // 2)
    m0 = np.concatenate([np.cos(angle(k0)), np.sin(angle(k0s))], axis=1)
    kk0 = np.concatenate([k0, k0s])
    s0 = np.where((kk0 == 0) | (kk0 == lon_total // 2), 1.0 / quarter, 2.0 / quarter)
    k2 = 4 * np.arange(quarter // 2) + 2
    m2 = np.concatenate([np.cos(angle(k2)), np.sin(angle(k2))], axis=1)
    kk2 = np.concatenate([k2, k2])
    s2 = np.full(quarter, 2.0 / quarter)
    k1 = 4 * np.arange(quarter) + 1
    cos1, sin1 = np.cos(angle(k1)), np.sin(angle(k1))
    m1 = np.concatenate(
        [np.concatenate([cos1, -sin1], axis=1), np.concatenate([-sin1, -cos1], axis=1)], axis=0
    )
    f1 = np.minimum(k1, lon_total - k1)
    kk1 = np.concatenate([f1, f1])
    s1 = np.full(2 * quarter, 1.0 / quarter)
    waves = np.concatenate([kk0, kk2, kk1]).astype(np.float32)
    scale = np.concatenate([s0 / 4, s2 / 4, s1 / 2]).astype(np.float32)
    return (m0, m2, m1), waves, scale


def damp_table(row_index, polar_rows, wave_numbers, lat_total, band_rows, lon_total):
    latitude_cos = jnp.sin(math.pi * (row_index.astype(jnp.float32) + 0.5) / lat_total)
    ratio = latitude_cos / math.sin(math.pi * band_rows / lat_total)
    wave_sine = jnp.sin(math.pi * wave_numbers / lon_total)
    safe_sine = jnp.where(wave_numbers > 0.5, wave_sine, 1.0)
    damping = jnp.where(
        wave_numbers[None, :] > 0.5, jnp.minimum(1.0, ratio[:, None] / safe_sine[None, :]), 1.0
    )
    listed = jnp.any(row_index[:, None] == polar_rows[None, :], axis=1)
    return jnp.where(listed[:, None], damping, 1.0)


def peer_copy(src, dst, send_sem, recv_sem, lat, lon):
    return pltpu.make_async_remote_copy(
        src_ref=src, dst_ref=dst, send_sem=send_sem, recv_sem=recv_sem,
        device_id=(lat, lon), device_id_type=MESH,
    )


def stencil_kernel(lat_n, lon_n, q, wind_u, wind_v, out, last_row, first_row, last_col, first_col,
                   south, north, west, east, send, recv):
    levels, rows, cols = q.shape
    lat, lon = lax.axis_index("lat"), lax.axis_index("lon")
    right, left = lax.rem(lon + 1, lon_n), lax.rem(lon + lon_n - 1, lon_n)
    has_up, has_down = lat < lat_n - 1, lat > 0
    barrier = pltpu.get_barrier_semaphore()
    for side in (left, right):
        pl.semaphore_signal(barrier, inc=1, device_id=(lat, side), device_id_type=MESH)

    @pl.when(has_up)
    def _():
        pl.semaphore_signal(barrier, inc=1, device_id=(lat + 1, lon), device_id_type=MESH)

    @pl.when(has_down)
    def _():
        pl.semaphore_signal(barrier, inc=1, device_id=(lat - 1, lon), device_id_type=MESH)

    lane = lax.broadcasted_iota(jnp.int32, (rows, 128), 1)
    right_tile = jnp.zeros((rows, 128), jnp.float32)
    left_tile = jnp.zeros((rows, 128), jnp.float32)
    for l in range(levels):
        right_tile = jnp.where(lane == l, q[l, :, cols - 1:cols], right_tile)
        left_tile = jnp.where(lane == l, q[l, :, 0:1], left_tile)
        last_row[l:l + 1, :] = q[l, rows - 1:rows, :]
        first_row[l:l + 1, :] = q[l, 0:1, :]
    last_col[...] = right_tile
    first_col[...] = left_tile
    pl.semaphore_wait(barrier, 2 + has_up.astype(jnp.int32) + has_down.astype(jnp.int32))
    go_right = peer_copy(last_col, west, send.at[0], recv.at[0], lat, right)
    go_left = peer_copy(first_col, east, send.at[1], recv.at[1], lat, left)
    go_up = peer_copy(last_row, south, send.at[2], recv.at[2], lat + 1, lon)
    go_down = peer_copy(first_row, north, send.at[3], recv.at[3], lat - 1, lon)
    go_right.start()
    go_left.start()

    @pl.when(has_up)
    def _():
        go_up.start()

    @pl.when(has_down)
    def _():
        go_down.start()

    @pl.when(has_up)
    def _():
        go_up.wait_send()
        go_down.wait_recv()

    @pl.when(jnp.logical_not(has_up))
    def _():
        north[...] = jnp.zeros_like(north)

    @pl.when(has_down)
    def _():
        go_down.wait_send()
        go_up.wait_recv()

    @pl.when(jnp.logical_not(has_down))
    def _():
        south[...] = jnp.zeros_like(south)

    go_right.wait()
    go_left.wait()
    for l in range(levels):
        x = q[l]
        east_side = jnp.concatenate([x[:, 1:], east[:, l:l + 1]], axis=1)
        west_side = jnp.concatenate([west[:, l:l + 1], x[:, :-1]], axis=1)
        north_side = jnp.concatenate([x[1:], north[l:l + 1]], axis=0)
        south_side = jnp.concatenate([south[l:l + 1], x[:-1]], axis=0)
        advect = wind_u[l] * (east_side - west_side) + wind_v[l] * (north_side - south_side)
        spread_sum = east_side + west_side + north_side + south_side - 4.0 * x
        out[l] = x - advect_coef * advect + diffuse_coef * spread_sum


def atmos_step(mesh_sizes, tracer_now, wind_u, wind_v):
    lat_n, lon_n = mesh_sizes
    levels, rows, cols = tracer_now.shape
    row_edge = pltpu.VMEM((levels, cols), jnp.float32)
    col_edge = pltpu.VMEM((rows, 128), jnp.float32)
    return pl.pallas_call(
        functools.partial(stencil_kernel, lat_n, lon_n),
        out_shape=jax.ShapeDtypeStruct(tracer_now.shape, jnp.float32),
        in_specs=[VMEM] * 3,
        out_specs=VMEM,
        scratch_shapes=[row_edge, row_edge, col_edge, col_edge] * 2
        + [pltpu.SemaphoreType.DMA((4,)), pltpu.SemaphoreType.DMA((4,))],
        compiler_params=params(0),
        name="stencil",
    )(tracer_now, wind_u, wind_v)


def dot3(x, high, low, contract):
    lines = x.shape[0]
    x_high = x.astype(jnp.bfloat16)
    x_low = (x - x_high.astype(jnp.float32)).astype(jnp.bfloat16)

    def one(a, b):
        return lax.dot_general(
            a, b, (((1,), (contract,)), ((), ())), preferred_element_type=jnp.float32
        )

    both = one(jnp.concatenate([x_high, x_low], axis=0), high)
    return (both[lines:] + one(x_high, low)) + both[:lines]


def filter_kernel(lat_n, band, slots, row_of, slot_of, listed, q, w, h0, l0, h2, l2, h1, l1, out,
                  hold, go, rx, ret, back, send, recv, back_send, back_recv):
    lat, lon = lax.axis_index("lat"), lax.axis_index("lon")
    levels, rows, cols = q.shape
    each = levels // 4
    lines = each * slots
    full, rest = cols // 128, cols % 128
    per = 128 // rest
    polar = jnp.logical_or(lat < band, lat >= lat_n - band)

    def pack(message, j):
        base = j * each
        for t in range(full):
            message[j, t * each:(t + 1) * each] = hold[base:base + each, :, t * 128:(t + 1) * 128]
        for g in range(each // per):
            message[j, full * each + g] = jnp.concatenate(
                [hold[base + g * per + i, :, full * 128:] for i in range(per)], axis=1
            )

    def unpack(message, j):
        base = j * each
        for t in range(full):
            hold[base:base + each, :, t * 128:(t + 1) * 128] = message[j, t * each:(t + 1) * each]
        for g in range(each // per):
            tails = message[j, full * each + g]
            for i in range(per):
                hold[base + g * per + i, :, full * 128:] = tails[:, i * rest:(i + 1) * rest]

    @pl.when(jnp.logical_not(polar))
    def _():
        out[...] = q[...]

    @pl.when(polar)
    def _():
        barrier = pltpu.get_barrier_semaphore()
        for d in (1, 2, 3):
            pl.semaphore_signal(
                barrier, inc=1, device_id=(lat, lax.rem(lon + d, 4)), device_id_type=MESH
            )
        for s in range(slots):
            hold[:, s:s + 1, :] = q[:, pl.ds(row_of[s], 1), :]
        for j in range(4):
            pack(go, j)
        pl.semaphore_wait(barrier, 3)
        there, home = [], []
        for d in (2, 3, 1):
            dest = lax.rem(lon + d, 4)
            copy = peer_copy(
                go.at[dest], rx.at[lon],
                send.at[d - 1], recv.at[d - 1], lat, dest,
            )
            copy.start()
            there.append(copy)
        rx[pl.ds(lon, 1)] = go[pl.ds(lon, 1)]
        for copy in there:
            copy.wait_recv()
        for j in range(4):
            unpack(rx, j)
        x = [hold[j * each:(j + 1) * each].reshape(lines, cols) for j in range(4)]
        even, odd = x[0] + x[2], x[1] + x[3]
        a, b = x[0] - x[2], x[1] - x[3]

        def weigh(coeffs, start):
            width = coeffs.shape[1]
            scaled = coeffs.reshape(each, slots, width) * w[:, start:start + width][None]
            return scaled.reshape(lines, width)

        f0 = weigh(dot3(even + odd, h0[...], l0[...], 0), 0)
        f2 = weigh(dot3(even - odd, h2[...], l2[...], 0), cols)
        f1 = dot3(a, h1[:cols], l1[:cols], 0) + dot3(b, h1[cols:], l1[cols:], 0)
        f1 = weigh(f1, 2 * cols)
        y0 = dot3(f0, h0[...], l0[...], 1)
        y2 = dot3(f2, h2[...], l2[...], 1)
        a = dot3(f1, h1[:cols], l1[:cols], 1)
        b = dot3(f1, h1[cols:], l1[cols:], 1)
        plus, minus = y0 + y2, y0 - y2
        for j, y in enumerate((plus + a, minus + b, plus - a, minus - b)):
            hold[j * each:(j + 1) * each] = y.reshape(each, slots, cols)
            pack(ret, j)
        for d in (2, 3, 1):
            dest = lax.rem(lon + d, 4)
            copy = peer_copy(
                ret.at[dest], back.at[lon],
                back_send.at[d - 1], back_recv.at[d - 1], lat, dest,
            )
            copy.start()
            home.append(copy)
        back[pl.ds(lon, 1)] = ret[pl.ds(lon, 1)]
        for copy in there:
            copy.wait_send()
        for copy in home:
            copy.wait()
        for j in range(4):
            unpack(back, j)
        for r in range(rows):
            kept = q[:, r:r + 1, :]
            filtered = hold[:, pl.ds(slot_of[r], 1), :]
            out[:, r:r + 1, :] = jnp.where(listed[r] > 0, filtered, kept)


def polar_filter(lat_n, band, slots, cid, q, plan, bases):
    levels, rows, cols = q.shape
    each = levels // 4
    smem = pl.BlockSpec(memory_space=pltpu.SMEM)
    sems = [pltpu.SemaphoreType.DMA((3,))] * 4
    whole = pltpu.VMEM((levels, slots, cols), jnp.float32)
    per = 128 // (cols % 128)
    planes = cols // 128 * each + each // per
    parts = pltpu.VMEM((4, planes, slots, 128), jnp.float32)
    row_of, slot_of, listed, weights = plan
    return pl.pallas_call(
        functools.partial(filter_kernel, lat_n, band, slots),
        out_shape=jax.ShapeDtypeStruct(q.shape, jnp.float32),
        in_specs=[smem] * 3 + [VMEM] * 8,
        out_specs=VMEM,
        scratch_shapes=[whole] + [parts] * 4 + sems,
        compiler_params=params(cid),
        name="polar_filter",
    )(row_of, slot_of, listed, q, weights, *bases)


AROUND = [(dy, dx) for dy in (-1, 0, 1) for dx in (-1, 0, 1) if (dy, dx) != (0, 0)]


def around_exchange(lat_n, lon_n, pieces, send, recv, fill):
    lat, lon = lax.axis_index("lat"), lax.axis_index("lon")
    has = {0: None, 1: lat < lat_n - 1, -1: lat > 0}

    def guarded(dy, action):
        if dy == 0:
            action()
        else:
            pl.when(has[dy])(action)

    def side(dx):
        return lax.rem(lon + dx + lon_n, lon_n)

    barrier = pltpu.get_barrier_semaphore()

    def greet(dy):
        for dx in (-1, 0, 1):
            if (dy, dx) != (0, 0):
                pl.semaphore_signal(
                    barrier, inc=1, device_id=(lat + dy, side(dx)), device_id_type=MESH
                )

    for dy in (0, 1, -1):
        guarded(dy, functools.partial(greet, dy))
    fill(has)
    pl.semaphore_wait(barrier, 2 + 3 * (has[1].astype(jnp.int32) + has[-1].astype(jnp.int32)))
    copies = {}
    for at, (dy, dx) in enumerate(AROUND):
        src, dst = pieces(dy, dx)
        copies[dy, dx] = peer_copy(src, dst, send.at[at], recv.at[at], lat + dy, side(dx))
    for dy in (0, 1, -1):
        group = [copies[dy, dx] for dx in (-1, 0, 1) if (dy, dx) != (0, 0)]

        def begin(group=group):
            for copy in group:
                copy.start()

        guarded(dy, begin)
    for dy in (0, 1, -1):
        group = [copies[dy, dx] for dx in (-1, 0, 1) if (dy, dx) != (0, 0)]
        other = [copies[-dy, dx] for dx in (-1, 0, 1) if (dy, dx) != (0, 0)]

        def end(group=group, other=other):
            for copy in group:
                copy.wait_send()
            for copy in other:
                copy.wait_recv()

        guarded(dy, end)


def rim_kernel(lat_n, lon_n, bottom, got, send, recv):
    at = {piece: index for index, piece in enumerate(AROUND)}
    rows = bottom.shape[1]
    start = {-1: 0, 0: 0, 1: rows - 8}

    def pieces(dy, dx):
        span = pl.ds(start[dy], rows if dy == 0 else 8)
        return bottom.at[:, span], got.at[at[dy, dx], :, span]

    around_exchange(lat_n, lon_n, pieces, send, recv, lambda has: None)


def rim_exchange(lat_n, lon_n, bottom):
    return pl.pallas_call(
        functools.partial(rim_kernel, lat_n, lon_n),
        out_shape=jax.ShapeDtypeStruct((8,) + bottom.shape, jnp.float32),
        in_specs=[VMEM],
        out_specs=VMEM,
        scratch_shapes=[pltpu.SemaphoreType.DMA((8,)), pltpu.SemaphoreType.DMA((8,))],
        compiler_params=params(2),
        name="rim",
    )(bottom)


def remap_kernel(table, row, col, out):
    fields, table_rows, width = table.shape
    blocks = width // 128
    column_blocks = row.shape[1] // 128

    def one(step, carry):
        i = pl.multiple_of(step // column_blocks * 8, 8)
        j = pl.multiple_of(step % column_blocks * 128, 128)
        r = row[pl.ds(i, 8), pl.ds(j, 128)]
        c = col[pl.ds(i, 8), pl.ds(j, 128)]
        key = r * blocks + c // 128
        lane = c % 128
        totals = [jnp.zeros((8, 128), jnp.float32)] * fields
        for tr in range(table_rows):
            for tb in range(blocks):
                hit = key == tr * blocks + tb
                for f in range(fields):
                    line = table[f, tr:tr + 1, tb * 128:(tb + 1) * 128]
                    wide = jnp.broadcast_to(line, (8, 128))
                    got = jnp.take_along_axis(wide, lane, axis=1, mode="promise_in_bounds")
                    totals[f] = jnp.where(hit, got, totals[f])
        for f in range(fields):
            out[f, pl.ds(i, 8), pl.ds(j, 128)] = totals[f]
        return carry

    lax.fori_loop(0, row.shape[0] // 8 * column_blocks, one, 0)


def remap(table, row, col):
    return pl.pallas_call(
        remap_kernel,
        out_shape=jax.ShapeDtypeStruct((table.shape[0],) + row.shape, jnp.float32),
        in_specs=[VMEM] * 3,
        out_specs=VMEM,
        compiler_params=params(),
        name="remap",
    )(table, row, col)


def ocean_kernel(lat_n, lon_n, temp, mask, air, out, ext, send, recv):
    level_count, rows, cols = temp.shape
    high, wide = rows + 16, cols + 256

    def fill(has):
        ext[0:level_count, 8:8 + rows, 128:128 + cols] = temp[...]
        ext[level_count, 8:8 + rows, 128:128 + cols] = mask[...].astype(jnp.float32)
        ext[level_count + 1:level_count + 3, 8:8 + rows, 128:128 + cols] = air[...]

        @pl.when(jnp.logical_not(has[1]))
        def _():
            ext[:, 8 + rows:, :] = jnp.zeros((level_count + 3, 8, wide), jnp.float32)

        @pl.when(jnp.logical_not(has[-1]))
        def _():
            ext[:, :8, :] = jnp.zeros((level_count + 3, 8, wide), jnp.float32)

    source_rows = {-1: (8, 8), 0: (8, rows), 1: (rows, 8)}
    target_rows = {-1: (8 + rows, 8), 0: (8, rows), 1: (0, 8)}
    source_cols = {-1: (128, 128), 0: (128, cols), 1: (cols, 128)}
    target_cols = {-1: (128 + cols, 128), 0: (128, cols), 1: (0, 128)}

    def pieces(dy, dx):
        def view(r, c):
            return ext.at[:, pl.ds(*r), pl.ds(*c)]

        return (
            view(source_rows[dy], source_cols[dx]),
            view(target_rows[dy], target_cols[dx]),
        )

    around_exchange(lat_n, lon_n, pieces, send, recv, fill)
    sea = ext[level_count]
    air_temp = ext[level_count + 1]
    gain = sea * flux_coef * ext[level_count + 2]

    def shifts(x):
        return (
            pltpu.roll(x, wide - 1, 1), pltpu.roll(x, 1, 1),
            pltpu.roll(x, high - 1, 0), pltpu.roll(x, 1, 0),
        )

    couplings = [ocean_diffuse * sea * s for s in shifts(sea)]
    total = couplings[0] + couplings[1] + couplings[2] + couplings[3]
    mix = vertical_mix * sea
    levels = [ext[l] for l in range(level_count)]
    for _ in range(OSTEPS):
        levels[0] = levels[0] + gain * (air_temp - levels[0])
        for l in range(level_count):
            t = levels[l]
            moved = shifts(t)
            flow = couplings[0] * (moved[0] - t)
            for k in range(1, 4):
                flow = flow + couplings[k] * (moved[k] - t)
            levels[l] = t + flow
        upper = [levels[0]] + levels[:-1]
        lower = levels[1:] + [levels[-1]]
        levels = [
            t + mix * (u + d - 2.0 * t) for t, u, d in zip(levels, upper, lower)
        ]
    for l in range(level_count):
        out[l] = levels[l][8:8 + rows, 128:128 + cols]


def ocean(lat_n, lon_n, temp, mask, air):
    level_count, rows, cols = temp.shape
    return pl.pallas_call(
        functools.partial(ocean_kernel, lat_n, lon_n),
        out_shape=jax.ShapeDtypeStruct(temp.shape, jnp.float32),
        in_specs=[VMEM] * 3,
        out_specs=VMEM,
        scratch_shapes=[
            pltpu.VMEM((level_count + 3, rows + 16, cols + 256), jnp.float32),
            pltpu.SemaphoreType.DMA((8,)),
            pltpu.SemaphoreType.DMA((8,)),
        ],
        compiler_params=params(3),
        name="ocean",
    )(temp, mask, air)


def rim_table(bottom, around, lat_place, lat_n):
    got = {piece: around[index] for index, piece in enumerate(AROUND)}
    north_row = jnp.concatenate(
        [got[-1, 1][:, :1, -1:], got[-1, 0][:, :1], got[-1, -1][:, :1, :1]], axis=2
    )
    south_row = jnp.concatenate(
        [got[1, 1][:, -1:, -1:], got[1, 0][:, -1:], got[1, -1][:, -1:, :1]], axis=2
    )
    middle = jnp.concatenate([got[0, 1][:, :, -1:], bottom, got[0, -1][:, :, :1]], axis=2)
    table = jnp.concatenate([south_row, middle, north_row], axis=1)
    width = table.shape[2]
    return jnp.pad(table, ((0, 0), (0, 0), (0, -width % 128)))


def per_device(tracer, wind_u, wind_v, ocean_temp, land_mask, remap_rows, remap_cols, polar_rows):
    levels, row_count, lon_local = tracer.shape
    lat_devices = lax.axis_size("lat")
    lon_devices = lax.axis_size("lon")
    sizes = (lat_devices, lon_devices)
    lat_total = row_count * lat_devices
    lon_total = lon_local * lon_devices
    band_devices = lat_devices // 8
    band_rows = band_devices * row_count
    lat_place = lax.axis_index("lat")
    lon_place = lax.axis_index("lon")
    matrices, waves, scale = make_bases(lon_total)
    bases = []
    for matrix in matrices:
        bases.extend(jnp.asarray(part) for part in split_basis(matrix))
    band_first = lax.broadcasted_iota(jnp.int32, (lat_devices, 1), 0) * row_count
    inside = (polar_rows[None, :] >= band_first) & (polar_rows[None, :] < band_first + row_count)
    most = jnp.max(jnp.sum(inside.astype(jnp.int32), axis=1))
    local_rows = jnp.arange(row_count, dtype=jnp.int32)
    own_rows = lat_place * row_count + local_rows
    listed = jnp.any(own_rows[:, None] == polar_rows[None, :], axis=1)
    before = (local_rows[None, :] < local_rows[:, None]) & listed[None, :]
    slot_of = jnp.sum(before.astype(jnp.int32), axis=1)

    filled = (slot_of[None, :] == local_rows[:, None]) & listed[None, :]
    row_of = jnp.sum(jnp.where(filled, local_rows[None, :], 0), axis=1)
    weights = (
        damp_table(
            lat_place * row_count + row_of, polar_rows, jnp.asarray(waves),
            lat_total, band_rows, lon_total,
        )
        * jnp.asarray(scale)[None, :]
    )
    listed = listed.astype(jnp.int32)

    def atmosphere(slots, cid, tracer_now):
        plan = (row_of[:slots], jnp.minimum(slot_of, slots - 1), listed, weights[:slots])
        for step in range(STEPS):
            if step > 0:
                tracer_now = atmos_step(sizes, tracer_now, wind_u, wind_v)
            tracer_now = polar_filter(
                lat_devices, band_devices, slots, cid, tracer_now, plan, bases
            )
        return tracer_now

    few = 16
    tracer_now = lax.cond(
        most <= few,
        functools.partial(atmosphere, few, 1),
        functools.partial(atmosphere, row_count, 4),
        atmos_step(sizes, tracer, wind_u, wind_v),
    )
    bottom = jnp.stack(
        [tracer_now[levels - 1], jnp.abs(wind_u[levels - 1]) + jnp.abs(wind_v[levels - 1]) + 0.5]
    )
    around = rim_exchange(lat_devices, lon_devices, bottom)
    table = rim_table(bottom, around, lat_place, lat_devices)
    local_row = remap_rows - lat_place * row_count + 1
    local_col = (remap_cols - lon_place * lon_local + 1) % lon_total
    air = remap(table, local_row, local_col)
    return (tracer_now, ocean(lat_devices, lon_devices, ocean_temp, land_mask, air))


def solution(mesh):
    in_specs = (
        P(None, "lat", "lon"),
        P(None, "lat", "lon"),
        P(None, "lat", "lon"),
        P(None, "lat", "lon"),
        P("lat", "lon"),
        P("lat", "lon"),
        P("lat", "lon"),
        P(),
    )
    out_specs = (P(None, "lat", "lon"), P(None, "lat", "lon"))
    return jax.shard_map(
        per_device, mesh=mesh, in_specs=in_specs, out_specs=out_specs, check_vma=False
    )
```

```python
import functools
import math

import jax
import jax.numpy as jnp
import ml_dtypes
import numpy as np
from jax import lax
from jax.experimental import pallas as pl
from jax.experimental.pallas import tpu as pltpu
from jax.sharding import PartitionSpec as P

STEPS = 2
OSTEPS = 2
MESH = pl.DeviceIdType.MESH
VMEM = pl.BlockSpec(memory_space=pltpu.VMEM)

advect_coef = 0.2
diffuse_coef = 0.1
flux_coef = 0.25
ocean_diffuse = 0.15
vertical_mix = 0.2


def params(cid=None):
    if cid is None:
        return pltpu.CompilerParams(vmem_limit_bytes=48 * 2**20)
    return pltpu.CompilerParams(
        collective_id=cid, has_side_effects=True, vmem_limit_bytes=48 * 2**20
    )


def split_basis(matrix):
    high = matrix.astype(ml_dtypes.bfloat16)
    low = (matrix - high.astype(np.float64)).astype(ml_dtypes.bfloat16)
    return high, low


def make_bases(lon_total):
    quarter = lon_total // 4
    n = np.arange(quarter)[:, None]

    def angle(k):
        return 2.0 * math.pi * ((n * k[None, :]) % lon_total) / lon_total

    k0 = 4 * np.arange(quarter // 2 + 1)
    k0s = 4 * np.arange(1, quarter // 2)
    m0 = np.concatenate([np.cos(angle(k0)), np.sin(angle(k0s))], axis=1)
    kk0 = np.concatenate([k0, k0s])
    s0 = np.where((kk0 == 0) | (kk0 == lon_total // 2), 1.0 / quarter, 2.0 / quarter)
    k2 = 4 * np.arange(quarter // 2) + 2
    m2 = np.concatenate([np.cos(angle(k2)), np.sin(angle(k2))], axis=1)
    kk2 = np.concatenate([k2, k2])
    s2 = np.full(quarter, 2.0 / quarter)
    k1 = 4 * np.arange(quarter) + 1
    cos1, sin1 = np.cos(angle(k1)), np.sin(angle(k1))
    m1 = np.concatenate(
        [np.concatenate([cos1, -sin1], axis=1), np.concatenate([-sin1, -cos1], axis=1)], axis=0
    )
    f1 = np.minimum(k1, lon_total - k1)
    kk1 = np.concatenate([f1, f1])
    s1 = np.full(2 * quarter, 1.0 / quarter)
    waves = np.concatenate([kk0, kk2, kk1]).astype(np.float32)
    scale = np.concatenate([s0 / 4, s2 / 4, s1 / 2]).astype(np.float32)
    return (m0, m2, m1), waves, scale


def damp_table(row_index, polar_rows, wave_numbers, lat_total, band_rows, lon_total):
    latitude_cos = jnp.sin(math.pi * (row_index.astype(jnp.float32) + 0.5) / lat_total)
    ratio = latitude_cos / math.sin(math.pi * band_rows / lat_total)
    wave_sine = jnp.sin(math.pi * wave_numbers / lon_total)
    safe_sine = jnp.where(wave_numbers > 0.5, wave_sine, 1.0)
    damping = jnp.where(
        wave_numbers[None, :] > 0.5, jnp.minimum(1.0, ratio[:, None] / safe_sine[None, :]), 1.0
    )
    listed = jnp.any(row_index[:, None] == polar_rows[None, :], axis=1)
    return jnp.where(listed[:, None], damping, 1.0)


def peer_copy(src, dst, send_sem, recv_sem, lat, lon):
    return pltpu.make_async_remote_copy(
        src_ref=src, dst_ref=dst, send_sem=send_sem, recv_sem=recv_sem,
        device_id=(lat, lon), device_id_type=MESH,
    )


def stencil_kernel(lat_n, lon_n, q, wind_u, wind_v, out, last_row, first_row, last_col, first_col,
                   south, north, west, east, send, recv):
    levels, rows, cols = q.shape
    lat, lon = lax.axis_index("lat"), lax.axis_index("lon")
    right, left = lax.rem(lon + 1, lon_n), lax.rem(lon + lon_n - 1, lon_n)
    has_up, has_down = lat < lat_n - 1, lat > 0
    barrier = pltpu.get_barrier_semaphore()
    for side in (left, right):
        pl.semaphore_signal(barrier, inc=1, device_id=(lat, side), device_id_type=MESH)

    @pl.when(has_up)
    def _():
        pl.semaphore_signal(barrier, inc=1, device_id=(lat + 1, lon), device_id_type=MESH)

    @pl.when(has_down)
    def _():
        pl.semaphore_signal(barrier, inc=1, device_id=(lat - 1, lon), device_id_type=MESH)

    lane = lax.broadcasted_iota(jnp.int32, (rows, 128), 1)
    right_tile = jnp.zeros((rows, 128), jnp.float32)
    left_tile = jnp.zeros((rows, 128), jnp.float32)
    for l in range(levels):
        right_tile = jnp.where(lane == l, q[l, :, cols - 1:cols], right_tile)
        left_tile = jnp.where(lane == l, q[l, :, 0:1], left_tile)
        last_row[l:l + 1, :] = q[l, rows - 1:rows, :]
        first_row[l:l + 1, :] = q[l, 0:1, :]
    last_col[...] = right_tile
    first_col[...] = left_tile
    pl.semaphore_wait(barrier, 2 + has_up.astype(jnp.int32) + has_down.astype(jnp.int32))
    go_right = peer_copy(last_col, west, send.at[0], recv.at[0], lat, right)
    go_left = peer_copy(first_col, east, send.at[1], recv.at[1], lat, left)
    go_up = peer_copy(last_row, south, send.at[2], recv.at[2], lat + 1, lon)
    go_down = peer_copy(first_row, north, send.at[3], recv.at[3], lat - 1, lon)
    go_right.start()
    go_left.start()

    @pl.when(has_up)
    def _():
        go_up.start()

    @pl.when(has_down)
    def _():
        go_down.start()

    @pl.when(has_up)
    def _():
        go_up.wait_send()
        go_down.wait_recv()

    @pl.when(jnp.logical_not(has_up))
    def _():
        north[...] = jnp.zeros_like(north)

    @pl.when(has_down)
    def _():
        go_down.wait_send()
        go_up.wait_recv()

    @pl.when(jnp.logical_not(has_down))
    def _():
        south[...] = jnp.zeros_like(south)

    go_right.wait()
    go_left.wait()
    for l in range(levels):
        x = q[l]
        east_side = jnp.concatenate([x[:, 1:], east[:, l:l + 1]], axis=1)
        west_side = jnp.concatenate([west[:, l:l + 1], x[:, :-1]], axis=1)
        north_side = jnp.concatenate([x[1:], north[l:l + 1]], axis=0)
        south_side = jnp.concatenate([south[l:l + 1], x[:-1]], axis=0)
        advect = wind_u[l] * (east_side - west_side) + wind_v[l] * (north_side - south_side)
        spread_sum = east_side + west_side + north_side + south_side - 4.0 * x
        out[l] = x - advect_coef * advect + diffuse_coef * spread_sum


def atmos_step(mesh_sizes, tracer_now, wind_u, wind_v):
    lat_n, lon_n = mesh_sizes
    levels, rows, cols = tracer_now.shape
    row_edge = pltpu.VMEM((levels, cols), jnp.float32)
    col_edge = pltpu.VMEM((rows, 128), jnp.float32)
    return pl.pallas_call(
        functools.partial(stencil_kernel, lat_n, lon_n),
        out_shape=jax.ShapeDtypeStruct(tracer_now.shape, jnp.float32),
        in_specs=[VMEM] * 3,
        out_specs=VMEM,
        scratch_shapes=[row_edge, row_edge, col_edge, col_edge] * 2
        + [pltpu.SemaphoreType.DMA((4,)), pltpu.SemaphoreType.DMA((4,))],
        compiler_params=params(0),
        name="stencil",
    )(tracer_now, wind_u, wind_v)


def dot3(x, high, low, contract):
    lines = x.shape[0]
    x_high = x.astype(jnp.bfloat16)
    x_low = (x - x_high.astype(jnp.float32)).astype(jnp.bfloat16)

    def one(a, b):
        return lax.dot_general(
            a, b, (((1,), (contract,)), ((), ())), preferred_element_type=jnp.float32
        )

    both = one(jnp.concatenate([x_high, x_low], axis=0), high)
    return (both[lines:] + one(x_high, low)) + both[:lines]


def filter_kernel(lat_n, band, slots, row_of, slot_of, listed, q, w, h0, l0, h2, l2, h1, l1, out,
                  hold, go, rx, ret, back, send, recv, back_send, back_recv):
    lat, lon = lax.axis_index("lat"), lax.axis_index("lon")
    levels, rows, cols = q.shape
    each = levels // 4
    lines = each * slots
    full, rest = cols // 128, cols % 128
    per = 128 // rest
    polar = jnp.logical_or(lat < band, lat >= lat_n - band)

    def pack(message, j):
        base = j * each
        for t in range(full):
            message[j, t * each:(t + 1) * each] = hold[base:base + each, :, t * 128:(t + 1) * 128]
        for g in range(each // per):
            message[j, full * each + g] = jnp.concatenate(
                [hold[base + g * per + i, :, full * 128:] for i in range(per)], axis=1
            )

    def unpack(message, j):
        base = j * each
        for t in range(full):
            hold[base:base + each, :, t * 128:(t + 1) * 128] = message[j, t * each:(t + 1) * each]
        for g in range(each // per):
            tails = message[j, full * each + g]
            for i in range(per):
                hold[base + g * per + i, :, full * 128:] = tails[:, i * rest:(i + 1) * rest]

    @pl.when(jnp.logical_not(polar))
    def _():
        out[...] = q[...]

    @pl.when(polar)
    def _():
        barrier = pltpu.get_barrier_semaphore()
        for d in (1, 2, 3):
            pl.semaphore_signal(
                barrier, inc=1, device_id=(lat, lax.rem(lon + d, 4)), device_id_type=MESH
            )
        for s in range(slots):
            hold[:, s:s + 1, :] = q[:, pl.ds(row_of[s], 1), :]
        for j in range(4):
            pack(go, j)
        pl.semaphore_wait(barrier, 3)
        there, home = [], []
        for d in (2, 3, 1):
            dest = lax.rem(lon + d, 4)
            copy = peer_copy(
                go.at[dest], rx.at[lon],
                send.at[d - 1], recv.at[d - 1], lat, dest,
            )
            copy.start()
            there.append(copy)
        rx[pl.ds(lon, 1)] = go[pl.ds(lon, 1)]
        for copy in there:
            copy.wait_recv()
        for j in range(4):
            unpack(rx, j)
        x = [hold[j * each:(j + 1) * each].reshape(lines, cols) for j in range(4)]
        even, odd = x[0] + x[2], x[1] + x[3]
        a, b = x[0] - x[2], x[1] - x[3]

        def weigh(coeffs, start):
            width = coeffs.shape[1]
            scaled = coeffs.reshape(each, slots, width) * w[:, start:start + width][None]
            return scaled.reshape(lines, width)

        f0 = weigh(dot3(even + odd, h0[...], l0[...], 0), 0)
        f2 = weigh(dot3(even - odd, h2[...], l2[...], 0), cols)
        f1 = dot3(a, h1[:cols], l1[:cols], 0) + dot3(b, h1[cols:], l1[cols:], 0)
        f1 = weigh(f1, 2 * cols)
        y0 = dot3(f0, h0[...], l0[...], 1)
        y2 = dot3(f2, h2[...], l2[...], 1)
        a = dot3(f1, h1[:cols], l1[:cols], 1)
        b = dot3(f1, h1[cols:], l1[cols:], 1)
        plus, minus = y0 + y2, y0 - y2
        for j, y in enumerate((plus + a, minus + b, plus - a, minus - b)):
            hold[j * each:(j + 1) * each] = y.reshape(each, slots, cols)
            pack(ret, j)
        for d in (2, 3, 1):
            dest = lax.rem(lon + d, 4)
            copy = peer_copy(
                ret.at[dest], back.at[lon],
                back_send.at[d - 1], back_recv.at[d - 1], lat, dest,
            )
            copy.start()
            home.append(copy)
        back[pl.ds(lon, 1)] = ret[pl.ds(lon, 1)]
        for copy in there:
            copy.wait_send()
        for copy in home:
            copy.wait()
        for j in range(4):
            unpack(back, j)
        for r in range(rows):
            kept = q[:, r:r + 1, :]
            filtered = hold[:, pl.ds(slot_of[r], 1), :]
            out[:, r:r + 1, :] = jnp.where(listed[r] > 0, filtered, kept)


def polar_filter(lat_n, band, slots, cid, q, plan, bases):
    levels, rows, cols = q.shape
    each = levels // 4
    smem = pl.BlockSpec(memory_space=pltpu.SMEM)
    sems = [pltpu.SemaphoreType.DMA((3,))] * 4
    whole = pltpu.VMEM((levels, slots, cols), jnp.float32)
    per = 128 // (cols % 128)
    planes = cols // 128 * each + each // per
    parts = pltpu.VMEM((4, planes, slots, 128), jnp.float32)
    row_of, slot_of, listed, weights = plan
    return pl.pallas_call(
        functools.partial(filter_kernel, lat_n, band, slots),
        out_shape=jax.ShapeDtypeStruct(q.shape, jnp.float32),
        in_specs=[smem] * 3 + [VMEM] * 8,
        out_specs=VMEM,
        scratch_shapes=[whole] + [parts] * 4 + sems,
        compiler_params=params(cid),
        name="polar_filter",
    )(row_of, slot_of, listed, q, weights, *bases)


AROUND = [(dy, dx) for dy in (-1, 0, 1) for dx in (-1, 0, 1) if (dy, dx) != (0, 0)]


def around_exchange(lat_n, lon_n, pieces, send, recv, fill):
    lat, lon = lax.axis_index("lat"), lax.axis_index("lon")
    has = {0: None, 1: lat < lat_n - 1, -1: lat > 0}

    def guarded(dy, action):
        if dy == 0:
            action()
        else:
            pl.when(has[dy])(action)

    def side(dx):
        return lax.rem(lon + dx + lon_n, lon_n)

    barrier = pltpu.get_barrier_semaphore()

    def greet(dy):
        for dx in (-1, 0, 1):
            if (dy, dx) != (0, 0):
                pl.semaphore_signal(
                    barrier, inc=1, device_id=(lat + dy, side(dx)), device_id_type=MESH
                )

    for dy in (0, 1, -1):
        guarded(dy, functools.partial(greet, dy))
    fill(has)
    pl.semaphore_wait(barrier, 2 + 3 * (has[1].astype(jnp.int32) + has[-1].astype(jnp.int32)))
    copies = {}
    for at, (dy, dx) in enumerate(AROUND):
        src, dst = pieces(dy, dx)
        copies[dy, dx] = peer_copy(src, dst, send.at[at], recv.at[at], lat + dy, side(dx))
    for dy in (0, 1, -1):
        group = [copies[dy, dx] for dx in (-1, 0, 1) if (dy, dx) != (0, 0)]

        def begin(group=group):
            for copy in group:
                copy.start()

        guarded(dy, begin)
    for dy in (0, 1, -1):
        group = [copies[dy, dx] for dx in (-1, 0, 1) if (dy, dx) != (0, 0)]
        other = [copies[-dy, dx] for dx in (-1, 0, 1) if (dy, dx) != (0, 0)]

        def end(group=group, other=other):
            for copy in group:
                copy.wait_send()
            for copy in other:
                copy.wait_recv()

        guarded(dy, end)


def rim_kernel(lat_n, lon_n, bottom, got, send, recv):
    at = {piece: index for index, piece in enumerate(AROUND)}
    rows = bottom.shape[1]
    start = {-1: 0, 0: 0, 1: rows - 8}

    def pieces(dy, dx):
        span = pl.ds(start[dy], rows if dy == 0 else 8)
        return bottom.at[:, span], got.at[at[dy, dx], :, span]

    around_exchange(lat_n, lon_n, pieces, send, recv, lambda has: None)


def rim_exchange(lat_n, lon_n, bottom):
    return pl.pallas_call(
        functools.partial(rim_kernel, lat_n, lon_n),
        out_shape=jax.ShapeDtypeStruct((8,) + bottom.shape, jnp.float32),
        in_specs=[VMEM],
        out_specs=VMEM,
        scratch_shapes=[pltpu.SemaphoreType.DMA((8,)), pltpu.SemaphoreType.DMA((8,))],
        compiler_params=params(2),
        name="rim",
    )(bottom)


def remap_kernel(table, row, col, out):
    fields, table_rows, width = table.shape
    blocks = width // 128
    column_blocks = row.shape[1] // 128

    def one(step, carry):
        i = pl.multiple_of(step // column_blocks * 8, 8)
        j = pl.multiple_of(step % column_blocks * 128, 128)
        r = row[pl.ds(i, 8), pl.ds(j, 128)]
        c = col[pl.ds(i, 8), pl.ds(j, 128)]
        key = r * blocks + c // 128
        lane = c % 128
        totals = [jnp.zeros((8, 128), jnp.float32)] * fields
        for tr in range(table_rows):
            for tb in range(blocks):
                hit = key == tr * blocks + tb
                for f in range(fields):
                    line = table[f, tr:tr + 1, tb * 128:(tb + 1) * 128]
                    wide = jnp.broadcast_to(line, (8, 128))
                    got = jnp.take_along_axis(wide, lane, axis=1, mode="promise_in_bounds")
                    totals[f] = jnp.where(hit, got, totals[f])
        for f in range(fields):
            out[f, pl.ds(i, 8), pl.ds(j, 128)] = totals[f]
        return carry

    lax.fori_loop(0, row.shape[0] // 8 * column_blocks, one, 0)


def remap(table, row, col):
    return pl.pallas_call(
        remap_kernel,
        out_shape=jax.ShapeDtypeStruct((table.shape[0],) + row.shape, jnp.float32),
        in_specs=[VMEM] * 3,
        out_specs=VMEM,
        compiler_params=params(),
        name="remap",
    )(table, row, col)


def ocean_kernel(lat_n, lon_n, temp, mask, air, out, ext, send, recv):
    level_count, rows, cols = temp.shape
    high, wide = rows + 16, cols + 256

    def fill(has):
        ext[0:level_count, 8:8 + rows, 128:128 + cols] = temp[...]
        ext[level_count, 8:8 + rows, 128:128 + cols] = mask[...].astype(jnp.float32)
        ext[level_count + 1:level_count + 3, 8:8 + rows, 128:128 + cols] = air[...]

        @pl.when(jnp.logical_not(has[1]))
        def _():
            ext[:, 8 + rows:, :] = jnp.zeros((level_count + 3, 8, wide), jnp.float32)

        @pl.when(jnp.logical_not(has[-1]))
        def _():
            ext[:, :8, :] = jnp.zeros((level_count + 3, 8, wide), jnp.float32)

    source_rows = {-1: (8, 8), 0: (8, rows), 1: (rows, 8)}
    target_rows = {-1: (8 + rows, 8), 0: (8, rows), 1: (0, 8)}
    source_cols = {-1: (128, 128), 0: (128, cols), 1: (cols, 128)}
    target_cols = {-1: (128 + cols, 128), 0: (128, cols), 1: (0, 128)}

    def pieces(dy, dx):
        def view(r, c):
            return ext.at[:, pl.ds(*r), pl.ds(*c)]

        return (
            view(source_rows[dy], source_cols[dx]),
            view(target_rows[dy], target_cols[dx]),
        )

    around_exchange(lat_n, lon_n, pieces, send, recv, fill)
    lane = lax.broadcasted_iota(jnp.int32, (high, 128), 1)
    sub = lax.broadcasted_iota(jnp.int32, (8, cols + 128), 0)

    def ring(f):
        sides = jnp.where(lane < 64, ext[f, :, 128 + cols:], ext[f, :, :128])
        x = jnp.concatenate([ext[f, :, 128:128 + cols], sides], axis=1)
        ends = jnp.where(sub < 4, x[8 + rows:], x[:8])
        return jnp.concatenate([x[8:8 + rows], ends], axis=0)

    sea = ring(level_count)
    air_temp = ring(level_count + 1)
    gain = sea * flux_coef * ring(level_count + 2)
    ring_high, ring_wide = rows + 8, cols + 128

    def shifts(x):
        return (
            pltpu.roll(x, ring_wide - 1, 1), pltpu.roll(x, 1, 1),
            pltpu.roll(x, ring_high - 1, 0), pltpu.roll(x, 1, 0),
        )

    couplings = [ocean_diffuse * sea * s for s in shifts(sea)]
    keep = 1.0 - (couplings[0] + couplings[1] + couplings[2] + couplings[3])
    mix = vertical_mix * sea
    levels = [ring(l) for l in range(level_count)]
    for _ in range(OSTEPS):
        levels[0] = levels[0] + gain * (air_temp - levels[0])
        for l in range(level_count):
            t = levels[l]
            moved = shifts(t)
            spread = keep * t
            for k in range(4):
                spread = spread + couplings[k] * moved[k]
            levels[l] = spread
        upper = [levels[0]] + levels[:-1]
        lower = levels[1:] + [levels[-1]]
        levels = [
            t + mix * (u + d - 2.0 * t) for t, u, d in zip(levels, upper, lower)
        ]
    for l in range(level_count):
        out[l] = levels[l][:rows, :cols]


def ocean(lat_n, lon_n, temp, mask, air):
    level_count, rows, cols = temp.shape
    return pl.pallas_call(
        functools.partial(ocean_kernel, lat_n, lon_n),
        out_shape=jax.ShapeDtypeStruct(temp.shape, jnp.float32),
        in_specs=[VMEM] * 3,
        out_specs=VMEM,
        scratch_shapes=[
            pltpu.VMEM((level_count + 3, rows + 16, cols + 256), jnp.float32),
            pltpu.SemaphoreType.DMA((8,)),
            pltpu.SemaphoreType.DMA((8,)),
        ],
        compiler_params=params(3),
        name="ocean",
    )(temp, mask, air)


def rim_table(bottom, around, lat_place, lat_n):
    got = {piece: around[index] for index, piece in enumerate(AROUND)}
    north_row = jnp.concatenate(
        [got[-1, 1][:, :1, -1:], got[-1, 0][:, :1], got[-1, -1][:, :1, :1]], axis=2
    )
    south_row = jnp.concatenate(
        [got[1, 1][:, -1:, -1:], got[1, 0][:, -1:], got[1, -1][:, -1:, :1]], axis=2
    )
    middle = jnp.concatenate([got[0, 1][:, :, -1:], bottom, got[0, -1][:, :, :1]], axis=2)
    table = jnp.concatenate([south_row, middle, north_row], axis=1)
    width = table.shape[2]
    return jnp.pad(table, ((0, 0), (0, 0), (0, -width % 128)))


def per_device(tracer, wind_u, wind_v, ocean_temp, land_mask, remap_rows, remap_cols, polar_rows):
    levels, row_count, lon_local = tracer.shape
    lat_devices = lax.axis_size("lat")
    lon_devices = lax.axis_size("lon")
    sizes = (lat_devices, lon_devices)
    lat_total = row_count * lat_devices
    lon_total = lon_local * lon_devices
    band_devices = lat_devices // 8
    band_rows = band_devices * row_count
    lat_place = lax.axis_index("lat")
    lon_place = lax.axis_index("lon")
    matrices, waves, scale = make_bases(lon_total)
    bases = []
    for matrix in matrices:
        bases.extend(jnp.asarray(part) for part in split_basis(matrix))
    band_first = lax.broadcasted_iota(jnp.int32, (lat_devices, 1), 0) * row_count
    inside = (polar_rows[None, :] >= band_first) & (polar_rows[None, :] < band_first + row_count)
    most = jnp.max(jnp.sum(inside.astype(jnp.int32), axis=1))
    local_rows = jnp.arange(row_count, dtype=jnp.int32)
    own_rows = lat_place * row_count + local_rows
    listed = jnp.any(own_rows[:, None] == polar_rows[None, :], axis=1)
    before = (local_rows[None, :] < local_rows[:, None]) & listed[None, :]
    slot_of = jnp.sum(before.astype(jnp.int32), axis=1)

    filled = (slot_of[None, :] == local_rows[:, None]) & listed[None, :]
    row_of = jnp.sum(jnp.where(filled, local_rows[None, :], 0), axis=1)
    weights = (
        damp_table(
            lat_place * row_count + row_of, polar_rows, jnp.asarray(waves),
            lat_total, band_rows, lon_total,
        )
        * jnp.asarray(scale)[None, :]
    )
    listed = listed.astype(jnp.int32)

    def atmosphere(slots, cid, tracer_now):
        plan = (row_of[:slots], jnp.minimum(slot_of, slots - 1), listed, weights[:slots])
        for step in range(STEPS):
            if step > 0:
                tracer_now = atmos_step(sizes, tracer_now, wind_u, wind_v)
            tracer_now = polar_filter(
                lat_devices, band_devices, slots, cid, tracer_now, plan, bases
            )
        return tracer_now

    few = 16
    tracer_now = lax.cond(
        most <= few,
        functools.partial(atmosphere, few, 1),
        functools.partial(atmosphere, row_count, 4),
        atmos_step(sizes, tracer, wind_u, wind_v),
    )
    bottom = jnp.stack(
        [tracer_now[levels - 1], jnp.abs(wind_u[levels - 1]) + jnp.abs(wind_v[levels - 1]) + 0.5]
    )
    around = rim_exchange(lat_devices, lon_devices, bottom)
    table = rim_table(bottom, around, lat_place, lat_devices)
    local_row = remap_rows - lat_place * row_count + 1
    local_col = (remap_cols - lon_place * lon_local + 1) % lon_total
    air = remap(table, local_row, local_col)
    return (tracer_now, ocean(lat_devices, lon_devices, ocean_temp, land_mask, air))


def solution(mesh):
    in_specs = (
        P(None, "lat", "lon"),
        P(None, "lat", "lon"),
        P(None, "lat", "lon"),
        P(None, "lat", "lon"),
        P("lat", "lon"),
        P("lat", "lon"),
        P("lat", "lon"),
        P(),
    )
    out_specs = (P(None, "lat", "lon"), P(None, "lat", "lon"))
    return jax.shard_map(
        per_device, mesh=mesh, in_specs=in_specs, out_specs=out_specs, check_vma=False
    )
```
